512 devices in a mesh: dp: 8 (over z), dap: 64 (over y, x, core).
Axes of the slice: x: 4, y: 8, z: 8, core: 2. Of those that a mesh axis runs over, the one named last changes fastest.
Arguments:
- pair_map: bfloat16 [4096, 512, 128], P(('dp', 'dap')), parts along dimension 0, may hold values from -3 to 3
- atom_feats: bfloat16 [49152, 128], P(('dp', 'dap')), parts along dimension 0, may hold values from -6 to 6
- atom_token: int32 [49152], P(('dp', 'dap')), parts along dimension 0, may hold values from 0 to 511, as said below
- atom_weight: bfloat16 [128, 384], replicated, may hold values from -0.5 to 0.5
- left_weight: bfloat16 [384, 128], replicated, may hold values from -0.109375 to 0.109375
- right_weight: bfloat16 [384, 128], replicated, may hold values from -0.109375 to 0.109375
- tri_proj: bfloat16 [2, 128, 512], replicated, may hold values from -0.5 to 0.5
- tri_gate: bfloat16 [2, 128, 128], replicated, may hold values from -1 to 1
- tri_out: bfloat16 [2, 128, 128], replicated, may hold values from -0.5 to 0.5
- tri_gains: float32 [2, 2, 128], replicated, may hold values from 0.1 to 1.9
Outputs:
- token_single: bfloat16 [4096, 384], P(('dp', 'dap')), parts along dimension 0
- pair_out: bfloat16 [4096, 512, 128], P(('dp', 'dap')), parts along dimension 0
The draws below stay inside these ranges and needn't reach their ends.
There are 8 independent parts, one for each index of `dp`. The reference program is written for one: setup_inputs(seed, part) draws one part's arguments, and reference() takes and returns one part's arrays. A program takes and returns all parts, laid end to end along the dimension named above; an argument that names none is the same for every part. Nothing has to cross between parts.
Inputs may be any that keep to these rules, and one draw needn't show every extreme that they name: Within each aligned block of 32 atoms atom_token never falls; the blocks are pieces of one crop's token list in order, stored on devices in a drawn order; every token of the crop has at least one atom; the atoms of one device belong to at most min(96, 512) distinct tokens, and in every draw the atoms of some device belong to exactly that many.
All inputs are finite; a program needn't handle non-finite values.
Results may differ from the reference program's by a relative error of at most 0.02.
Values may be sent and summed in bfloat16 or wider, within the bound.
No kernel may reach another device: no remote copies, remote signals or barrier semaphores. Data moves between devices by JAX's collectives and lax.ppermute only.
A program may use at most 64 MiB of HBM per device.

```python
import jax
import jax.numpy as jnp
from jax import lax

C = 128
CS = 384
CA = 128
ATOM_BLOCK = 32
N = 512
ATOM_DEV = 96
ATOMS = 6144


def draw_pair_map(key, part):
    key = jax.random.fold_in(key, 11)
    values = jnp.clip(jax.random.normal(key, (N, N, C), jnp.float32), -3.0, 3.0)
    return values.astype(jnp.bfloat16)


def draw_atom_token(key, part):
    key = jax.random.fold_in(key, 7)
    cut_key = jax.random.fold_in(key, 1)
    order_key = jax.random.fold_in(key, 2)
    place_key = jax.random.fold_in(key, 3)
    block_total = ATOMS // ATOM_BLOCK
    device_total = ATOMS // ATOM_DEV
    per_device = ATOM_DEV // ATOM_BLOCK
    dense = min(ATOM_DEV, N)
    run_index = jax.random.randint(jax.random.fold_in(place_key, 1), (), 1, device_total, dtype=jnp.int32)
    start = run_index * ATOM_DEV
    spare = ATOMS - ATOM_DEV
    picks = jax.random.permutation(cut_key, spare)[:N - dense].astype(jnp.int32)
    outside = jnp.where(picks < start, picks + 1, picks + ATOM_DEV).astype(jnp.int32)
    inside = (start + jnp.arange(1, dense, dtype=jnp.int32)).astype(jnp.int32)
    boundaries = jnp.sort(jnp.concatenate([outside, inside]))
    positions = jnp.arange(ATOMS, dtype=jnp.int32)
    ordered = jnp.searchsorted(boundaries, positions, side='right').astype(jnp.int32)
    blocks = ordered.reshape(block_total, ATOM_BLOCK)
    order = jax.random.permutation(order_key, block_total).astype(jnp.int32)
    target = block_total // 2
    where_first = jnp.argmax((order == 0).astype(jnp.int32)).astype(jnp.int32)
    held = order[target]
    order = order.at[where_first].set(held)
    order = order.at[target].set(jnp.int32(0))
    middle_device = target // per_device
    offset = jax.random.randint(jax.random.fold_in(place_key, 2), (), 0, device_total - 1, dtype=jnp.int32)
    host = (middle_device + 1 + offset) % device_total
    for step in range(per_device):
        wanted = run_index * per_device + step
        slot = host * per_device + step
        where_now = jnp.argmax((order == wanted).astype(jnp.int32)).astype(jnp.int32)
        current = order[slot]
        order = order.at[where_now].set(current)
        order = order.at[slot].set(wanted)
    return blocks[order].reshape(ATOMS).astype(jnp.int32)


def levels(own_key, shape, shards, low, largest):
    def one(dim, blocks):
        draws = jax.random.uniform(jax.random.fold_in(jax.random.fold_in(own_key, 6), dim), (blocks,), jnp.float32, low / len(shards), largest / len(shards))
        return jnp.repeat(jnp.exp(draws), shape[dim] // blocks).reshape((-1,) + (1,) * (len(shape) - dim - 1))

    factor_of = one(*shards[0])
    for cut in shards[1:]:
        factor_of = factor_of * one(*cut)
    return factor_of


def scatter_about(rng, extent, scale, limit, pieces=(), held_as=jnp.bfloat16):
    array = scale * jax.random.normal(rng, extent, jnp.float32)
    if pieces:
        array = array * levels(rng, extent, pieces, -0.22, 0.18)
    return jnp.clip(array, -limit, limit).astype(held_as)


def setup_inputs(seed: int = 0, part: int = 0) -> dict:
    arg_keys = jax.random.split(jax.random.key(seed), 11)
    part_keys = jax.random.split(jax.random.fold_in(arg_keys[10], part), 11)
    pair_map = draw_pair_map(jax.random.fold_in(jax.random.fold_in(arg_keys[10], part), 71), part)
    atom_feats = scatter_about(part_keys[1], (ATOMS, CA), 1.0, 6.0, ((0, 64),))
    atom_token = draw_atom_token(jax.random.fold_in(jax.random.fold_in(arg_keys[10], part), 71), part)
    atom_weight = scatter_about(arg_keys[3], (CA, CS), CA ** -0.5, 0.5)
    left_weight = scatter_about(arg_keys[4], (CS, C), (8 * CS) ** -0.5, 0.109375)
    right_weight = scatter_about(arg_keys[5], (CS, C), (8 * CS) ** -0.5, 0.109375)
    tri_proj = scatter_about(arg_keys[6], (2, C, 4 * C), C ** -0.5, 0.5)
    tri_gate = scatter_about(arg_keys[7], (2, C, C), (C // 4) ** -0.5, 1.0)
    tri_out = scatter_about(arg_keys[8], (2, C, C), C ** -0.5, 0.5)
    tri_gains = jnp.clip(1.0 + 0.18 * jax.random.normal(arg_keys[9], (2, 2, C), jnp.float32), 0.1, 1.9)
    return dict(pair_map=pair_map, atom_feats=atom_feats, atom_token=atom_token, atom_weight=atom_weight, left_weight=left_weight, right_weight=right_weight, tri_proj=tri_proj, tri_gate=tri_gate, tri_out=tri_out, tri_gains=tri_gains)


EPS = 1e-05

def layer_norm(values, gain_vec, norm_axis):
    average = lax.optimization_barrier(jnp.mean(values, axis=norm_axis, keepdims=True))
    centred = values - average
    variance = lax.optimization_barrier(jnp.mean(centred * centred, axis=norm_axis, keepdims=True))
    return centred * lax.rsqrt(variance + EPS) * gain_vec

def triangle(pair_in, proj, gate, out, gains, incoming):
    normed = layer_norm(pair_in.astype(jnp.float32), gains[0], -1).astype(jnp.bfloat16)
    flattened = normed.reshape(N * N, C)
    projected = jnp.dot(flattened, proj, preferred_element_type=jnp.float32).reshape(N, N, 4 * C)
    left_ops = (jax.nn.sigmoid(projected[..., :C]) * projected[..., C:2 * C]).astype(jnp.bfloat16)
    right_ops = (jax.nn.sigmoid(projected[..., 2 * C:3 * C]) * projected[..., 3 * C:]).astype(jnp.bfloat16)
    gating = jax.nn.sigmoid(jnp.dot(flattened, gate, preferred_element_type=jnp.float32)).reshape(N, N, C)
    if incoming:
        product = jnp.einsum('kic,kjc->ijc', left_ops.astype(jnp.float32), right_ops.astype(jnp.float32))
    else:
        product = jnp.einsum('ikc,jkc->ijc', left_ops.astype(jnp.float32), right_ops.astype(jnp.float32))
    product = product.astype(jnp.bfloat16)
    normed_out = layer_norm(product.astype(jnp.float32), gains[1], -1).astype(jnp.bfloat16)
    update = jnp.dot(normed_out.reshape(N * N, C), out, preferred_element_type=jnp.float32).reshape(N, N, C)
    return (pair_in.astype(jnp.float32) + gating * update).astype(jnp.bfloat16)

def reference(pair_map, atom_feats, atom_token, atom_weight, left_weight, right_weight, tri_proj, tri_gate, tri_out, tri_gains):
    hidden = jax.nn.relu(jnp.dot(atom_feats, atom_weight, preferred_element_type=jnp.float32)).astype(jnp.bfloat16)
    sums = jax.ops.segment_sum(hidden.astype(jnp.float32), atom_token, num_segments=N)
    counts = jax.ops.segment_sum(jnp.ones((ATOMS,), jnp.float32), atom_token, num_segments=N)
    token_single = (sums / counts[:, None]).astype(jnp.bfloat16)
    left = jnp.dot(token_single, left_weight, preferred_element_type=jnp.float32).astype(jnp.bfloat16)
    right = jnp.dot(token_single, right_weight, preferred_element_type=jnp.float32).astype(jnp.bfloat16)
    current = (pair_map.astype(jnp.float32) + left.astype(jnp.float32)[:, None, :] + right.astype(jnp.float32)[None, :, :]).astype(jnp.bfloat16)
    for layer_index in range(2):
        current = triangle(current, tri_proj[layer_index], tri_gate[layer_index], tri_out[layer_index], tri_gains[layer_index], layer_index == 1)
    return (token_single, current)
```

```python
import jax
import jax.numpy as jnp
from jax import lax
from jax.experimental import pallas as pl
from jax.experimental.pallas import tpu as pltpu
from jax.sharding import PartitionSpec as P

EPS = 1e-05
F32, BF16 = jnp.float32, jnp.bfloat16
NT = (((1,), (1,)), ((), ()))
TN = (((0,), (0,)), ((), ()))
VMEM_LIMIT = 44 * 2**20


def mm(a, b, dims=(((1,), (0,)), ((), ()))):
    return lax.dot_general(a, b, dims, preferred_element_type=F32)


def sigmoid(x):
    return 0.5 * jnp.tanh(0.5 * x) + 0.5


def column(row, width):
    n = row.shape[1]
    tile = jnp.broadcast_to(row, (128, n)).T
    return jnp.concatenate([tile] * (width // 128), axis=1)


def norm_rows(x, gain):
    n = x.shape[0]
    centred = x - jnp.sum(x, axis=0, keepdims=True) * (1.0 / n)
    variance = jnp.sum(centred * centred, axis=0, keepdims=True) * (1.0 / n)
    return centred * lax.rsqrt(variance + EPS) * gain


def pool(feats_ref, tok_ref, weight_ref, tokens):
    atoms = feats_ref.shape[0]
    chunk = 512
    total = None
    for at in range(0, atoms, chunk):
        hidden = mm(feats_ref[at : at + chunk, :], weight_ref[...])
        hidden = jnp.maximum(hidden, 0.0).astype(BF16)
        hidden = jnp.concatenate([hidden, jnp.ones((chunk, 128), BF16)], axis=1)
        own = lax.broadcasted_iota(jnp.int32, (tokens, chunk), 0)
        picked = jnp.where(own == tok_ref[:, at : at + chunk], 1.0, 0.0).astype(BF16)
        part = mm(picked, hidden)
        total = part if total is None else total + part
    return total


def pool_kernel(feats_ref, tok_ref, weight_ref, out_ref):
    out_ref[...] = pool(feats_ref, tok_ref, weight_ref, out_ref.shape[0])


def put_row(s_ref, r, value):
    for t in range(s_ref.shape[0]):
        s_ref[t, pl.ds(r, value.shape[0], stride=8), :] = value[:, t * 128 : t * 128 + 128]


def get_row(s_ref, r, c):
    return jnp.concatenate(
        [s_ref[t, pl.ds(r, c, stride=8), :] for t in range(s_ref.shape[0])], axis=1
    )


def fill(s_ref, x_ref):
    for t in range(s_ref.shape[0]):
        s_ref[t] = x_ref[:, :, t * 128 : t * 128 + 128].reshape(-1, 128).astype(F32)


def operands(normed, proj_t, r, sa_ref, sb_ref):
    c = normed.shape[0]
    p = mm(proj_t, normed)
    put_row(sa_ref, r, sigmoid(p[:c]) * p[c : 2 * c])
    put_row(sb_ref, r, sigmoid(p[2 * c : 3 * c]) * p[3 * c :])


def pack(sa_ref, sb_ref, u_ref):
    n = u_ref.shape[0]
    for s_ref, at in ((sa_ref, 0), (sb_ref, 16)):
        for t in range(s_ref.shape[0]):
            u_ref[:, at : at + 16, t * 128 : t * 128 + 128] = (
                s_ref[t].reshape(n, 16, 128).astype(BF16)
            )


def first_kernel(
    idx_ref, psum_ref, feats_ref, tok_ref, weight_ref, wl_ref, wr_ref, pair_ref, proj_ref, gain_ref,
    single_ref, z_ref, n_ref, u_ref, ts_ref, sa_ref, sb_ref,
):
    rows, tokens, c = pair_ref.shape
    cs = wl_ref.shape[0]
    total = psum_ref[...] + pool(feats_ref, tok_ref, weight_ref, tokens)
    counts = total[:, cs:]
    single = jnp.concatenate(
        [total[:, at : at + 128] / counts for at in range(0, cs, 128)], axis=1
    )
    ts_ref[...] = single
    right = mm(single.astype(BF16), wr_ref[...]).astype(BF16).astype(F32)
    start = pl.multiple_of(idx_ref[0] * 8, 8)
    own = ts_ref[pl.ds(start, 8), :].astype(BF16)
    single_ref[...] = own
    left = mm(own, wl_ref[...]).astype(BF16).astype(F32)
    gain = column(gain_ref[...], tokens)
    proj_t = proj_ref[...].T
    for r in range(rows):
        z = (pair_ref[r].astype(F32) + left[r : r + 1, :] + right).astype(BF16)
        z = z.T
        z_ref[r] = z
        normed = norm_rows(z.astype(F32), gain).astype(BF16)
        n_ref[r] = normed
        operands(normed, proj_t, r, sa_ref, sb_ref)
    pack(sa_ref, sb_ref, u_ref)


def gate_kernel(n_ref, gate_ref, out_ref):
    gate_t = gate_ref[...].T
    for r in range(n_ref.shape[0]):
        out_ref[r] = sigmoid(mm(gate_t, n_ref[r]))


def product_kernel(dims, v_ref, r_ref):
    n, _, length = v_ref.shape
    a = v_ref[:, 0:16, :].astype(F32)
    b = v_ref[:, 16:32, :].astype(F32)
    out = []
    for ch in range(2):
        ac = a[:, ch * 8 : ch * 8 + 8, :].reshape(n * 8, length).astype(BF16)
        bc = b[:, ch * 8 : ch * 8 + 8, :].reshape(n * 8, length).astype(BF16)
        out.append(mm(ac, bc, dims).reshape(n, 8, length))
    r_ref[...] = jnp.concatenate(out, axis=1).astype(BF16)


def update_row(r, s_ref, out_t, gain, gating_ref, z_ref):
    c = out_t.shape[0]
    x = get_row(s_ref, r, c)
    normed = norm_rows(x, gain).astype(BF16)
    return z_ref[r].astype(F32) + gating_ref[r] * mm(out_t, normed)


def middle_kernel(
    x_ref, gating_ref, z_ref, out_ref, gain_out_ref, proj_ref, gain_in_ref,
    znew_ref, n_ref, u_ref, s_ref, sa_ref, sb_ref,
):
    rows, c, tokens = z_ref.shape
    fill(s_ref, x_ref)
    gain_out = column(gain_out_ref[...], tokens)
    gain_in = column(gain_in_ref[...], tokens)
    out_t = out_ref[...].T
    proj_t = proj_ref[...].T
    for r in range(rows):
        z = update_row(r, s_ref, out_t, gain_out, gating_ref, z_ref).astype(BF16)
        znew_ref[r] = z
        normed = norm_rows(z.astype(F32), gain_in).astype(BF16)
        n_ref[r] = normed
        operands(normed, proj_t, r, sa_ref, sb_ref)
    pack(sa_ref, sb_ref, u_ref)


def last_kernel(x_ref, gating_ref, z_ref, out_ref, gain_out_ref, pair_ref, s_ref):
    rows, c, tokens = z_ref.shape
    fill(s_ref, x_ref)
    gain_out = column(gain_out_ref[...], tokens)
    out_t = out_ref[...].T
    for r in range(rows):
        z = update_row(r, s_ref, out_t, gain_out, gating_ref, z_ref).astype(BF16)
        pair_ref[r] = z.T


def call(body, outs, args, scratch=(), name=None, flops=0, bytes_=0):
    specs = [
        pl.BlockSpec(memory_space=pltpu.SMEM if a.ndim == 1 else pltpu.VMEM) for a in args
    ]
    return pl.pallas_call(
        body,
        out_shape=outs,
        in_specs=specs,
        out_specs=jax.tree.map(lambda _: pl.BlockSpec(memory_space=pltpu.VMEM), outs),
        scratch_shapes=list(scratch),
        compiler_params=pltpu.CompilerParams(vmem_limit_bytes=VMEM_LIMIT),
        cost_estimate=pl.CostEstimate(flops=flops, bytes_accessed=bytes_, transcendentals=0),
        name=name,
    )(*args)


def local(
    pair_map, atom_feats, atom_token, atom_weight, left_weight, right_weight,
    tri_proj, tri_gate, tri_out, tri_gains,
):
    rows, tokens, c = pair_map.shape
    atoms = atom_feats.shape[0]
    cs = atom_weight.shape[1]
    n = lax.axis_size("dap")
    shape = jax.ShapeDtypeStruct
    me = lax.axis_index("dap").astype(jnp.int32).reshape(1)

    ny, nx = 8, 4
    groups_y = [[(y * nx + x) * 2 + k for y in range(ny)] for x in range(nx) for k in range(2)]
    groups_x = [[(y * nx + x) * 2 + k for x in range(nx)] for y in range(ny) for k in range(2)]
    tok = atom_token.reshape(1, atoms)
    tok = jnp.concatenate([tok // 32, tok % 32], axis=0).astype(BF16)
    tok = jnp.pad(tok, ((0, 14), (0, c - atoms)))
    packed = jnp.concatenate([atom_feats, tok], axis=0)

    def spread(v, count, groups):
        v = jnp.broadcast_to(v[None], (count,) + v.shape)
        return lax.all_to_all(
            v, "dap", split_axis=0, concat_axis=0, tiled=True, axis_index_groups=groups
        )

    got = spread(packed, ny, groups_y)
    got = spread(got.reshape(-1, c), nx, groups_x).reshape(ny * nx, atoms + 16, c)
    feats = got[:, :atoms, :].reshape(ny * nx * atoms, c)
    codes = got[:, atoms : atoms + 2, :atoms].astype(jnp.int32)
    toks = (codes[:, 0, :] * 32 + codes[:, 1, :]).reshape(1, ny * nx * atoms)
    swap = [(d, d ^ 1) for d in range(n)]
    feats_other = lax.ppermute(feats, "dap", swap)
    toks_other = lax.ppermute(toks, "dap", swap)
    psum = call(
        pool_kernel, shape((tokens, cs + 128), F32), (feats, toks, atom_weight),
        name="pool_half", flops=3_000_000_000, bytes_=2_000_000,
    )
    big = pltpu.VMEM((tokens // 128, rows * c, 128), F32)
    token_single, z, normed, sent = call(
        first_kernel,
        (
            shape((rows, cs), BF16),
            shape((rows, c, tokens), BF16),
            shape((rows, c, tokens), BF16),
            shape((n, 32, tokens), BF16),
        ),
        (me, psum, feats_other, toks_other, atom_weight, left_weight, right_weight, pair_map,
         tri_proj[0], tri_gains[0, 0:1]),
        [pltpu.VMEM((tokens, cs), F32), big, big],
        name="first", flops=4_000_000_000, bytes_=8_000_000,
    )

    def exchange(v):
        return lax.all_to_all(v, "dap", split_axis=0, concat_axis=0, tiled=True)

    for layer in range(2):
        got = exchange(sent)
        gating = call(
            gate_kernel, shape((rows, c, tokens), F32), (normed, tri_gate[layer]),
            name=f"gating{layer}", flops=200_000_000, bytes_=3_000_000,
        )
        dims = NT if layer == 0 else TN
        prod = call(
            lambda v, r, dims=dims: product_kernel(dims, v, r),
            shape((n, 16, tokens), BF16), (got,),
            name=f"product{layer}", flops=1_000_000_000, bytes_=3_000_000,
        )
        prod = exchange(prod)
        if layer == 0:
            z, normed, sent = call(
                middle_kernel,
                (
                    shape((rows, c, tokens), BF16),
                    shape((rows, c, tokens), BF16),
                    shape((n, 32, tokens), BF16),
                ),
                (prod, gating, z, tri_out[0], tri_gains[0, 1:2], tri_proj[1], tri_gains[1, 0:1]),
                [big, big, big],
                name="middle", flops=1_000_000_000, bytes_=8_000_000,
            )
        else:
            pair = call(
                last_kernel, shape((rows, tokens, c), BF16),
                (prod, gating, z, tri_out[1], tri_gains[1, 1:2]),
                [big],
                name="last", flops=200_000_000, bytes_=5_000_000,
            )
    return token_single, pair


def solution(mesh):
    placed = (
        P(("dp", "dap"), None, None),
        P(("dp", "dap"), None),
        P(("dp", "dap")),
        P(),
        P(),
        P(),
        P(),
        P(),
        P(),
        P(),
    )
    return jax.shard_map(
        local,
        mesh=mesh,
        in_specs=placed,
        out_specs=(P(("dp", "dap"), None), P(("dp", "dap"), None, None)),
        check_vma=False,
    )
```

```python
import jax
import jax.numpy as jnp
from jax import lax
from jax.experimental import pallas as pl
from jax.experimental.pallas import tpu as pltpu
from jax.sharding import PartitionSpec as P

EPS = 1e-05
F32, BF16 = jnp.float32, jnp.bfloat16
NT = (((1,), (1,)), ((), ()))
TN = (((0,), (0,)), ((), ()))
VMEM_LIMIT = 16 * 2**20


def mm(a, b, dims=(((1,), (0,)), ((), ()))):
    return lax.dot_general(a, b, dims, preferred_element_type=F32)


def sigmoid(x):
    return 0.5 * jnp.tanh(0.5 * x) + 0.5


def column(row, width):
    n = row.shape[1]
    tile = jnp.broadcast_to(row, (128, n)).T
    return jnp.concatenate([tile] * (width // 128), axis=1)


def norm_rows(x, gain):
    n = x.shape[0]
    centred = x - jnp.sum(x, axis=0, keepdims=True) * (1.0 / n)
    variance = jnp.sum(centred * centred, axis=0, keepdims=True) * (1.0 / n)
    return centred * lax.rsqrt(variance + EPS) * gain


def pool(packed_ref, weight_ref, tokens):
    blocks, rows, _ = packed_ref.shape
    atoms = rows - 16
    some = 8
    total = None
    for at in range(0, blocks, some):
        feats = packed_ref[at : at + some, 0:atoms, :].reshape(some * atoms, -1)
        hidden = jnp.maximum(mm(feats, weight_ref[...]), 0.0).astype(BF16)
        hidden = jnp.concatenate([hidden, jnp.ones((some * atoms, 128), BF16)], axis=1)
        toks = []
        for k in range(at, at + some):
            codes = packed_ref[k, atoms:rows, :].astype(F32)
            toks.append((codes[0:1, :atoms] * 32.0 + codes[1:2, :atoms]).astype(jnp.int32))
        toks = jnp.concatenate(toks, axis=1)
        own = lax.broadcasted_iota(jnp.int32, (tokens, some * atoms), 0)
        part = mm(jnp.where(own == toks, 1.0, 0.0).astype(BF16), hidden)
        total = part if total is None else total + part
    return total


def pool_kernel(packed_ref, weight_ref, out_ref):
    out_ref[...] = pool(packed_ref, weight_ref, out_ref.shape[0])


def put_row(s_ref, r, value):
    for t in range(s_ref.shape[0]):
        s_ref[t, pl.ds(r, value.shape[0], stride=8), :] = value[:, t * 128 : t * 128 + 128]


def get_row(s_ref, r, c):
    return jnp.concatenate(
        [s_ref[t, pl.ds(r, c, stride=8), :] for t in range(s_ref.shape[0])], axis=1
    )


def fill(s_ref, x_ref):
    for t in range(s_ref.shape[0]):
        s_ref[t] = x_ref[:, :, t * 128 : t * 128 + 128].reshape(-1, 128).astype(F32)


def operands(normed, proj_t, r, sa_ref, sb_ref):
    c = normed.shape[0]
    p = mm(proj_t, normed)
    put_row(sa_ref, r, sigmoid(p[:c]) * p[c : 2 * c])
    put_row(sb_ref, r, sigmoid(p[2 * c : 3 * c]) * p[3 * c :])


def pack(sa_ref, sb_ref, u_ref):
    n = u_ref.shape[0]
    for s_ref, at in ((sa_ref, 0), (sb_ref, 16)):
        for t in range(s_ref.shape[0]):
            u_ref[:, at : at + 16, t * 128 : t * 128 + 128] = (
                s_ref[t].reshape(n, 16, 128).astype(BF16)
            )


def first_kernel(
    idx_ref, psum_ref, packed_ref, weight_ref, wl_ref, wr_ref, pair_ref, proj_ref, gain_ref,
    single_ref, z_out, u_ref, ts_ref, sa_ref, sb_ref, z_ref, sem,
):
    rows, tokens, c = pair_ref.shape
    cs = wl_ref.shape[0]
    total = psum_ref[...] + pool(packed_ref, weight_ref, tokens)
    counts = total[:, cs:]
    single = jnp.concatenate(
        [total[:, at : at + 128] / counts for at in range(0, cs, 128)], axis=1
    )
    ts_ref[...] = single
    right = mm(single.astype(BF16), wr_ref[...]).astype(BF16).astype(F32)
    start = pl.multiple_of(idx_ref[0] * 8, 8)
    own = ts_ref[pl.ds(start, 8), :].astype(BF16)
    single_ref[...] = own
    left = mm(own, wl_ref[...]).astype(BF16).astype(F32)
    gain = column(gain_ref[...], tokens)
    proj_t = proj_ref[...].T
    for r in range(rows):
        z = (pair_ref[r].astype(F32) + left[r : r + 1, :] + right).astype(BF16)
        z = z.T
        z_ref[r] = z
        normed = norm_rows(z.astype(F32), gain).astype(BF16)
        operands(normed, proj_t, r, sa_ref, sb_ref)
    copy = pltpu.make_async_copy(z_ref, z_out, sem)
    copy.start()
    pack(sa_ref, sb_ref, u_ref)
    copy.wait()


def gate_kernel(z_in, gate_ref, gain_ref, out_ref, z_ref, sem):
    rows, _, tokens = z_ref.shape
    copy = pltpu.make_async_copy(z_in, z_ref, sem)
    copy.start()
    gate_t = gate_ref[...].T
    gain = column(gain_ref[...], tokens)
    copy.wait()
    for r in range(rows):
        z = z_ref[r]
        normed = norm_rows(z.astype(F32), gain).astype(BF16)
        out_ref[r] = sigmoid(mm(gate_t, normed)).astype(BF16)
        out_ref[rows + r] = z


def product_kernel(dims, v_ref, r_ref):
    n, _, length = v_ref.shape
    a = v_ref[:, 0:16, :].astype(F32)
    b = v_ref[:, 16:32, :].astype(F32)
    out = []
    for ch in range(2):
        ac = a[:, ch * 8 : ch * 8 + 8, :].reshape(n * 8, length).astype(BF16)
        bc = b[:, ch * 8 : ch * 8 + 8, :].reshape(n * 8, length).astype(BF16)
        out.append(mm(ac, bc, dims).reshape(n, 8, length))
    r_ref[...] = jnp.concatenate(out, axis=1).astype(BF16)


def update_row(r, s_ref, out_t, gain, held_ref):
    c = out_t.shape[0]
    x = get_row(s_ref, r, c)
    normed = norm_rows(x, gain).astype(BF16)
    rows = held_ref.shape[0] // 2
    gating, z = held_ref[r].astype(F32), held_ref[rows + r].astype(F32)
    return (z + gating * mm(out_t, normed)).astype(BF16)


def middle_kernel(
    x_ref, held_ref, out_ref, gain_out_ref, proj_ref, gain_in_ref,
    z_out, u_ref, s_ref, sa_ref, sb_ref, z_ref, sem,
):
    rows, c, tokens = z_ref.shape
    fill(s_ref, x_ref)
    gain_out = column(gain_out_ref[...], tokens)
    gain_in = column(gain_in_ref[...], tokens)
    out_t = out_ref[...].T
    proj_t = proj_ref[...].T
    for r in range(rows):
        z = update_row(r, s_ref, out_t, gain_out, held_ref)
        z_ref[r] = z
        normed = norm_rows(z.astype(F32), gain_in).astype(BF16)
        operands(normed, proj_t, r, sa_ref, sb_ref)
    copy = pltpu.make_async_copy(z_ref, z_out, sem)
    copy.start()
    pack(sa_ref, sb_ref, u_ref)
    copy.wait()


def last_kernel(x_ref, held_ref, out_ref, gain_out_ref, pair_ref, s_ref):
    rows, tokens, c = pair_ref.shape
    fill(s_ref, x_ref)
    gain_out = column(gain_out_ref[...], tokens)
    out_t = out_ref[...].T
    for r in range(rows):
        z = update_row(r, s_ref, out_t, gain_out, held_ref)
        pair_ref[r] = z.T


def call(body, outs, args, scratch=(), name=None, flops=0, bytes_=0, far_in=(), far_out=()):
    specs = [
        pl.BlockSpec(
            memory_space=pltpu.HBM if k in far_in else pltpu.SMEM if a.ndim == 1 else pltpu.VMEM
        )
        for k, a in enumerate(args)
    ]
    places = [
        pl.BlockSpec(memory_space=pltpu.HBM if k in far_out else pltpu.VMEM)
        for k in range(len(outs))
    ]
    return pl.pallas_call(
        body,
        out_shape=outs,
        in_specs=specs,
        out_specs=places,
        scratch_shapes=list(scratch),
        compiler_params=pltpu.CompilerParams(vmem_limit_bytes=VMEM_LIMIT),
        cost_estimate=pl.CostEstimate(flops=flops, bytes_accessed=bytes_, transcendentals=0),
        name=name,
    )(*args)


def local(
    pair_map, atom_feats, atom_token, atom_weight, left_weight, right_weight,
    tri_proj, tri_gate, tri_out, tri_gains,
):
    rows, tokens, c = pair_map.shape
    atoms = atom_feats.shape[0]
    cs = atom_weight.shape[1]
    n = lax.axis_size("dap")
    shape = jax.ShapeDtypeStruct
    me = lax.axis_index("dap").astype(jnp.int32).reshape(1)

    ny, nx = 8, 4
    groups_y = [[(y * nx + x) * 2 + k for y in range(ny)] for x in range(nx) for k in range(2)]
    groups_x = [[(y * nx + x) * 2 + k for x in range(nx)] for y in range(ny) for k in range(2)]
    tok = atom_token.reshape(1, atoms)
    tok = jnp.concatenate([tok // 32, tok % 32], axis=0).astype(BF16)
    tok = jnp.pad(tok, ((0, 14), (0, c - atoms)))
    packed = jnp.concatenate([atom_feats, tok], axis=0)

    got = lax.all_to_all(
        jnp.broadcast_to(packed[None], (ny,) + packed.shape), "dap",
        split_axis=0, concat_axis=0, tiled=True, axis_index_groups=groups_y,
    )
    got = lax.all_gather(got, "dap", axis=0, tiled=True, axis_index_groups=groups_x)
    other = lax.ppermute(got, "dap", [(d, d ^ 1) for d in range(n)])
    (psum,) = call(
        pool_kernel, (shape((tokens, cs + 128), F32),), (got, atom_weight),
        name="pool_half", flops=3_000_000_000, bytes_=2_000_000,
    )
    big = pltpu.VMEM((tokens // 128, rows * c, 128), F32)
    held = [pltpu.VMEM((rows, c, tokens), BF16), pltpu.SemaphoreType.DMA]
    z_shape = shape((rows, c, tokens), BF16)
    sent_shape = shape((n, 32, tokens), BF16)
    token_single, z, sent = call(
        first_kernel,
        (shape((rows, cs), BF16), z_shape, sent_shape),
        (me, psum, other, atom_weight, left_weight, right_weight, pair_map,
         tri_proj[0], tri_gains[0, 0:1]),
        [pltpu.VMEM((tokens, cs), F32), big, big, *held],
        name="first", flops=4_000_000_000, bytes_=8_000_000, far_out=(1,),
    )

    def exchange(v):
        return lax.all_to_all(v, "dap", split_axis=0, concat_axis=0, tiled=True)

    for layer in range(2):
        got = exchange(sent)
        (kept,) = call(
            gate_kernel, (shape((2 * rows, c, tokens), BF16),),
            (z, tri_gate[layer], tri_gains[layer, 0:1]), held,
            name=f"gating{layer}", flops=200_000_000, bytes_=3_000_000, far_in=(0,),
        )
        dims = NT if layer == 0 else TN
        (prod,) = call(
            lambda v, r, dims=dims: product_kernel(dims, v, r),
            (shape((n, 16, tokens), BF16),), (got,),
            name=f"product{layer}", flops=1_000_000_000, bytes_=3_000_000,
        )
        prod = exchange(prod)
        if layer == 0:
            z, sent = call(
                middle_kernel, (z_shape, sent_shape),
                (prod, kept, tri_out[0], tri_gains[0, 1:2], tri_proj[1], tri_gains[1, 0:1]),
                [big, big, big, *held],
                name="middle", flops=1_000_000_000, bytes_=8_000_000, far_out=(0,),
            )
        else:
            (pair,) = call(
                last_kernel, (shape((rows, tokens, c), BF16),),
                (prod, kept, tri_out[1], tri_gains[1, 1:2]),
                [big],
                name="last", flops=200_000_000, bytes_=5_000_000,
            )
    return token_single, pair


def solution(mesh):
    placed = (
        P(("dp", "dap"), None, None),
        P(("dp", "dap"), None),
        P(("dp", "dap")),
        P(),
        P(),
        P(),
        P(),
        P(),
        P(),
        P(),
    )
    return jax.shard_map(
        local,
        mesh=mesh,
        in_specs=placed,
        out_specs=(P(("dp", "dap"), None), P(("dp", "dap"), None, None)),
        check_vma=False,
    )
```

```python
import jax
import jax.numpy as jnp
from jax import lax
from jax.experimental import pallas as pl
from jax.experimental.pallas import tpu as pltpu
from jax.sharding import PartitionSpec as P

EPS = 1e-05
F32, BF16 = jnp.float32, jnp.bfloat16
NT = (((1,), (1,)), ((), ()))
TN = (((0,), (0,)), ((), ()))


def mm(a, b, dims=(((1,), (0,)), ((), ()))):
    return lax.dot_general(a, b, dims, preferred_element_type=F32)


def sigmoid(x):
    return 0.5 * jnp.tanh(0.5 * x) + 0.5


def column(row, width):
    n = row.shape[1]
    tile = jnp.broadcast_to(row, (128, n)).T
    return jnp.concatenate([tile] * (width // 128), axis=1)


def norm_rows(x, gain):
    n = x.shape[0]
    centred = x - jnp.sum(x, axis=0, keepdims=True) * (1.0 / n)
    variance = jnp.sum(centred * centred, axis=0, keepdims=True) * (1.0 / n)
    return centred * lax.rsqrt(variance + EPS) * gain


def pack_kernel(feats_in, tok_in, out_ref, feats_ref, tok_ref, sem_feats, sem_tok):
    copies = [
        pltpu.make_async_copy(feats_in, feats_ref, sem_feats),
        pltpu.make_async_copy(tok_in, tok_ref, sem_tok),
    ]
    for copy in copies:
        copy.start()
    for copy in copies:
        copy.wait()
    atoms, c = feats_ref.shape
    tok = jnp.concatenate([tok_ref[...], jnp.zeros((1, c - atoms), jnp.int32)], axis=1)
    row = lax.broadcasted_iota(jnp.int32, (16, c), 0)
    codes = jnp.where(row == 0, tok >> 5, jnp.where(row == 1, tok & 31, 0))
    block = jnp.concatenate([feats_ref[...], codes.astype(F32).astype(BF16)], axis=0)
    for k in range(out_ref.shape[0]):
        out_ref[k] = block


def pool(packed_ref, weight_ref, tokens):
    blocks, rows, _ = packed_ref.shape
    atoms = rows - 16
    some = 8
    total = None
    for at in range(0, blocks, some):
        feats = packed_ref[at : at + some, 0:atoms, :].reshape(some * atoms, -1)
        hidden = jnp.maximum(mm(feats, weight_ref[...]), 0.0).astype(BF16)
        hidden = jnp.concatenate([hidden, jnp.ones((some * atoms, 128), BF16)], axis=1)
        toks = []
        for k in range(at, at + some):
            codes = packed_ref[k, atoms:rows, :].astype(F32)
            toks.append((codes[0:1, :atoms] * 32.0 + codes[1:2, :atoms]).astype(jnp.int32))
        toks = jnp.concatenate(toks, axis=1)
        own = lax.broadcasted_iota(jnp.int32, (tokens, some * atoms), 0)
        part = mm(jnp.where(own == toks, 1.0, 0.0).astype(BF16), hidden)
        total = part if total is None else total + part
    return total


def put_row(s_ref, r, value):
    for t in range(s_ref.shape[0]):
        s_ref[t, pl.ds(r, value.shape[0], stride=8), :] = value[:, t * 128 : t * 128 + 128]


def get_row(s_ref, r, c):
    return jnp.concatenate(
        [s_ref[t, pl.ds(r, c, stride=8), :] for t in range(s_ref.shape[0])], axis=1
    )


def fill(s_ref, x_ref):
    for t in range(s_ref.shape[0]):
        s_ref[t] = x_ref[:, :, t * 128 : t * 128 + 128].reshape(-1, 128).astype(F32)


def operands(normed, half_proj_t, r, sa_ref, sb_ref):
    c = normed.shape[0]
    p = mm(half_proj_t, normed)
    put_row(sa_ref, r, jnp.tanh(p[:c]) * p[c : 2 * c] + p[c : 2 * c])
    put_row(sb_ref, r, jnp.tanh(p[2 * c : 3 * c]) * p[3 * c :] + p[3 * c :])


def pack(sa_ref, sb_ref, u_ref):
    n = u_ref.shape[0]
    for s_ref, at in ((sa_ref, 0), (sb_ref, 16)):
        for t in range(s_ref.shape[0]):
            u_ref[:, at : at + 16, t * 128 : t * 128 + 128] = (
                s_ref[t].reshape(n, 16, 128).astype(BF16)
            )


def first_kernel(
    idx_ref, packed_ref, weight_ref, wl_ref, wr_ref, pair_ref, proj_ref, gain_ref,
    single_ref, z_out, u_ref, ts_ref, sa_ref, sb_ref, z_ref, sem,
):
    rows, tokens, c = pair_ref.shape
    cs = wl_ref.shape[0]
    total = pool(packed_ref, weight_ref, tokens)
    counts = total[:, cs:]
    single = jnp.concatenate(
        [total[:, at : at + 128] / counts for at in range(0, cs, 128)], axis=1
    )
    ts_ref[...] = single
    right = mm(single.astype(BF16), wr_ref[...]).astype(BF16).astype(F32)
    start = pl.multiple_of(idx_ref[0] * 8, 8)
    own = ts_ref[pl.ds(start, 8), :].astype(BF16)
    single_ref[...] = own
    left = mm(own, wl_ref[...]).astype(BF16).astype(F32)
    gain = column(gain_ref[...], tokens)
    half_proj_t = (proj_ref[...].astype(F32) * 0.5).astype(BF16).T
    for r in range(rows):
        z = (pair_ref[r].astype(F32) + left[r : r + 1, :] + right).astype(BF16)
        z = z.T
        z_ref[r] = z
        normed = norm_rows(z.astype(F32), gain).astype(BF16)
        operands(normed, half_proj_t, r, sa_ref, sb_ref)
    copy = pltpu.make_async_copy(z_ref, z_out, sem)
    copy.start()
    pack(sa_ref, sb_ref, u_ref)
    copy.wait()


def gate_kernel(z_in, gate_ref, gain_ref, out_ref, z_ref, sem):
    rows, _, tokens = z_ref.shape
    copy = pltpu.make_async_copy(z_in, z_ref, sem)
    copy.start()
    gate_t = gate_ref[...].T
    gain = column(gain_ref[...], tokens)
    copy.wait()
    for r in range(rows):
        z = z_ref[r]
        normed = norm_rows(z.astype(F32), gain).astype(BF16)
        out_ref[r] = sigmoid(mm(gate_t, normed)).astype(BF16)
        out_ref[rows + r] = z


def product_kernel(dims, v_ref, r_ref):
    n, _, length = v_ref.shape
    a = v_ref[:, 0:16, :].astype(F32)
    b = v_ref[:, 16:32, :].astype(F32)
    out = []
    for ch in range(2):
        ac = a[:, ch * 8 : ch * 8 + 8, :].reshape(n * 8, length).astype(BF16)
        bc = b[:, ch * 8 : ch * 8 + 8, :].reshape(n * 8, length).astype(BF16)
        out.append(mm(ac, bc, dims).reshape(n, 8, length))
    r_ref[...] = jnp.concatenate(out, axis=1).astype(BF16)


def update_row(r, s_ref, out_t, gain, held_ref):
    c = out_t.shape[0]
    x = get_row(s_ref, r, c)
    normed = norm_rows(x, gain).astype(BF16)
    rows = held_ref.shape[0] // 2
    gating, z = held_ref[r].astype(F32), held_ref[rows + r].astype(F32)
    return (z + gating * mm(out_t, normed)).astype(BF16)


def middle_kernel(
    x_ref, held_ref, out_ref, gain_out_ref, proj_ref, gain_in_ref,
    z_out, u_ref, s_ref, sa_ref, sb_ref, z_ref, sem,
):
    rows, c, tokens = z_ref.shape
    fill(s_ref, x_ref)
    gain_out = column(gain_out_ref[...], tokens)
    gain_in = column(gain_in_ref[...], tokens)
    out_t = out_ref[...].T
    half_proj_t = (proj_ref[...].astype(F32) * 0.5).astype(BF16).T
    for r in range(rows):
        z = update_row(r, s_ref, out_t, gain_out, held_ref)
        z_ref[r] = z
        normed = norm_rows(z.astype(F32), gain_in).astype(BF16)
        operands(normed, half_proj_t, r, sa_ref, sb_ref)
    copy = pltpu.make_async_copy(z_ref, z_out, sem)
    copy.start()
    pack(sa_ref, sb_ref, u_ref)
    copy.wait()


def last_kernel(x_ref, held_ref, out_ref, gain_out_ref, pair_ref, s_ref):
    rows, tokens, c = pair_ref.shape
    fill(s_ref, x_ref)
    gain_out = column(gain_out_ref[...], tokens)
    out_t = out_ref[...].T
    for r in range(rows):
        z = update_row(r, s_ref, out_t, gain_out, held_ref)
        pair_ref[r] = z.T


def call(
    body, outs, args, scratch=(), name=None, flops=0, bytes_=0, far_in=(), far_out=(), vmem=16
):
    specs = [
        pl.BlockSpec(
            memory_space=pltpu.HBM if k in far_in else pltpu.SMEM if a.ndim == 1 else pltpu.VMEM
        )
        for k, a in enumerate(args)
    ]
    places = [
        pl.BlockSpec(memory_space=pltpu.HBM if k in far_out else pltpu.VMEM)
        for k in range(len(outs))
    ]
    return pl.pallas_call(
        body,
        out_shape=outs,
        in_specs=specs,
        out_specs=places,
        scratch_shapes=list(scratch),
        compiler_params=pltpu.CompilerParams(vmem_limit_bytes=vmem * 2**20),
        cost_estimate=pl.CostEstimate(flops=flops, bytes_accessed=bytes_, transcendentals=0),
        name=name,
    )(*args)


def local(
    pair_map, atom_feats, atom_token, atom_weight, left_weight, right_weight,
    tri_proj, tri_gate, tri_out, tri_gains,
):
    rows, tokens, c = pair_map.shape
    atoms = atom_feats.shape[0]
    cs = atom_weight.shape[1]
    n = lax.axis_size("dap")
    shape = jax.ShapeDtypeStruct
    me = lax.axis_index("dap").astype(jnp.int32).reshape(1)

    ny, nx = 8, 4
    groups_y = [[(y * nx + x) * 2 + k for y in range(ny)] for x in range(nx) for k in range(2)]
    groups_xk = [[y * nx * 2 + k for k in range(nx * 2)] for y in range(ny)]
    (packed,) = call(
        pack_kernel, (shape((ny, atoms + 16, c), BF16),), (atom_feats, atom_token.reshape(1, atoms)),
        [pltpu.VMEM((atoms, c), BF16), pltpu.VMEM((1, atoms), jnp.int32)]
        + [pltpu.SemaphoreType.DMA] * 2,
        name="packed_atoms", bytes_=300_000, far_in=(0, 1), vmem=60,
    )
    got = lax.all_to_all(
        packed, "dap", split_axis=0, concat_axis=0, tiled=True, axis_index_groups=groups_y
    )
    got = lax.all_gather(got, "dap", axis=0, tiled=True, axis_index_groups=groups_xk)
    big = pltpu.VMEM((tokens // 128, rows * c, 128), F32)
    held = [pltpu.VMEM((rows, c, tokens), BF16), pltpu.SemaphoreType.DMA]
    z_shape = shape((rows, c, tokens), BF16)
    sent_shape = shape((n, 32, tokens), BF16)
    token_single, z, sent = call(
        first_kernel,
        (shape((rows, cs), BF16), z_shape, sent_shape),
        (me, got, atom_weight, left_weight, right_weight, pair_map,
         tri_proj[0], tri_gains[0, 0:1]),
        [pltpu.VMEM((tokens, cs), F32), big, big, *held],
        name="first", flops=4_000_000_000, bytes_=8_000_000, far_out=(1,), vmem=32,
    )

    def exchange(v):
        return lax.all_to_all(v, "dap", split_axis=0, concat_axis=0, tiled=True)

    for layer in range(2):
        got = exchange(sent)
        (kept,) = call(
            gate_kernel, (shape((2 * rows, c, tokens), BF16),),
            (z, tri_gate[layer], tri_gains[layer, 0:1]), held,
            name=f"gating{layer}", flops=200_000_000, bytes_=3_000_000, far_in=(0,),
        )
        dims = NT if layer == 0 else TN
        (prod,) = call(
            lambda v, r, dims=dims: product_kernel(dims, v, r),
            (shape((n, 16, tokens), BF16),), (got,),
            name=f"product{layer}", flops=1_000_000_000, bytes_=3_000_000,
        )
        prod = exchange(prod)
        if layer == 0:
            z, sent = call(
                middle_kernel, (z_shape, sent_shape),
                (prod, kept, tri_out[0], tri_gains[0, 1:2], tri_proj[1], tri_gains[1, 0:1]),
                [big, big, big, *held],
                name="middle", flops=1_000_000_000, bytes_=8_000_000, far_out=(0,), vmem=32,
            )
        else:
            (pair,) = call(
                last_kernel, (shape((rows, tokens, c), BF16),),
                (prod, kept, tri_out[1], tri_gains[1, 1:2]),
                [big],
                name="last", flops=200_000_000, bytes_=5_000_000,
            )
    return token_single, pair


def solution(mesh):
    placed = (
        P(("dp", "dap"), None, None),
        P(("dp", "dap"), None),
        P(("dp", "dap")),
        P(),
        P(),
        P(),
        P(),
        P(),
        P(),
        P(),
    )
    return jax.shard_map(
        local,
        mesh=mesh,
        in_specs=placed,
        out_specs=(P(("dp", "dap"), None), P(("dp", "dap"), None, None)),
        check_vma=False,
    )
```

```python
import functools

import jax
import jax.numpy as jnp
from jax import lax
from jax.experimental import pallas as pl
from jax.experimental.pallas import tpu as pltpu
from jax.sharding import PartitionSpec as P

EPS = 1e-05
GROUP = 4
F32, BF16 = jnp.float32, jnp.bfloat16
NT = (((1,), (1,)), ((), ()))
TN = (((0,), (0,)), ((), ()))


def mm(a, b, dims=(((1,), (0,)), ((), ()))):
    return lax.dot_general(a, b, dims, preferred_element_type=F32)


def sigmoid(x):
    return 0.5 * jnp.tanh(0.5 * x) + 0.5


def column(row, width):
    n = row.shape[1]
    tile = jnp.broadcast_to(row, (128, n)).T
    return jnp.concatenate([tile] * (width // 128), axis=1)


def norm_rows(x, gain):
    n = x.shape[0]
    centred = x - jnp.sum(x, axis=0, keepdims=True) * (1.0 / n)
    variance = jnp.sum(centred * centred, axis=0, keepdims=True) * (1.0 / n)
    return centred * lax.rsqrt(variance + EPS) * gain


def pack_kernel(feats_in, tok_in, out_ref, feats_ref, tok_ref, sem_feats, sem_tok):
    copies = [
        pltpu.make_async_copy(feats_in, feats_ref, sem_feats),
        pltpu.make_async_copy(tok_in, tok_ref, sem_tok),
    ]
    for copy in copies:
        copy.start()
    for copy in copies:
        copy.wait()
    atoms, c = feats_ref.shape
    tok = jnp.concatenate([tok_ref[...], jnp.zeros((1, c - atoms), jnp.int32)], axis=1)
    row = lax.broadcasted_iota(jnp.int32, (16, c), 0)
    codes = jnp.where(row == 0, tok >> 5, jnp.where(row == 1, tok & 31, 0))
    block = jnp.concatenate([feats_ref[...], codes.astype(F32).astype(BF16)], axis=0)
    for k in range(out_ref.shape[0]):
        out_ref[k] = block


def pool(packed_ref, weight_ref, tokens):
    blocks, rows, _ = packed_ref.shape
    atoms = rows - 16
    some = 8
    total = None
    for at in range(0, blocks, some):
        feats = packed_ref[at : at + some, 0:atoms, :].reshape(some * atoms, -1)
        hidden = jnp.maximum(mm(feats, weight_ref[...]), 0.0).astype(BF16)
        hidden = jnp.concatenate([hidden, jnp.ones((some * atoms, 128), BF16)], axis=1)
        toks = []
        for k in range(at, at + some):
            codes = packed_ref[k, atoms:rows, :].astype(F32)
            toks.append((codes[0:1, :atoms] * 32.0 + codes[1:2, :atoms]).astype(jnp.int32))
        toks = jnp.concatenate(toks, axis=1)
        own = lax.broadcasted_iota(jnp.int32, (tokens, some * atoms), 0)
        part = mm(jnp.where(own == toks, 1.0, 0.0).astype(BF16), hidden)
        total = part if total is None else total + part
    return total


def pool_kernel(packed_ref, weight_ref, out_ref):
    out_ref[...] = pool(packed_ref, weight_ref, out_ref.shape[0])


def put_row(s_ref, r, value):
    for t in range(s_ref.shape[0]):
        s_ref[t, pl.ds(r, value.shape[0], stride=8), :] = value[:, t * 128 : t * 128 + 128]


def get_row(s_ref, r, c):
    return jnp.concatenate(
        [s_ref[t, pl.ds(r, c, stride=8), :] for t in range(s_ref.shape[0])], axis=1
    )


def fill(s_ref, x_ref):
    for t in range(s_ref.shape[0]):
        s_ref[t] = x_ref[:, :, t * 128 : t * 128 + 128].reshape(-1, 128).astype(F32)


def operands(normed, half_proj_t, at, sa_ref, sb_ref):
    c = normed.shape[0]
    length = sa_ref.shape[0] * 128
    for s_ref, block in ((sa_ref, 0), (sb_ref, 2)):
        p = mm(half_proj_t[block * c : (block + 2) * c], normed)
        p = jnp.tanh(p[:c]) * p[c:] + p[c:]
        for k in range(normed.shape[1] // length):
            put_row(s_ref, at + k, p[:, k * length : (k + 1) * length])


def pack(sa_ref, sb_ref, u_ref):
    n = u_ref.shape[0]
    for s_ref, at in ((sa_ref, 0), (sb_ref, 16)):
        for t in range(s_ref.shape[0]):
            u_ref[:, at : at + 16, t * 128 : t * 128 + 128] = (
                s_ref[t].reshape(n, 16, 128).astype(BF16)
            )


def first_kernel(
    idx_ref, psum_ref, packed_ref, weight_ref, wl_ref, wr_ref, pair_ref, proj_ref, gain_ref,
    single_ref, z_out, u_ref, ts_ref, sa_ref, sb_ref, z_ref, sem,
):
    rows, tokens, c = pair_ref.shape
    cs = wl_ref.shape[0]
    total = psum_ref[...] + pool(packed_ref, weight_ref, tokens)
    counts = total[:, cs:]
    single = jnp.concatenate(
        [total[:, at : at + 128] / counts for at in range(0, cs, 128)], axis=1
    )
    ts_ref[...] = single
    right = mm(single.astype(BF16), wr_ref[...]).astype(BF16).astype(F32)
    start = pl.multiple_of(idx_ref[0] * 8, 8)
    own = ts_ref[pl.ds(start, 8), :].astype(BF16)
    single_ref[...] = own
    left = mm(own, wl_ref[...]).astype(BF16).astype(F32)
    gain = column(gain_ref[0, 0:1, :], GROUP * tokens)
    half_proj_t = (proj_ref[0].astype(F32) * 0.5).astype(BF16).T
    for at in range(0, rows, GROUP):
        some = range(at, at + GROUP)
        z = [
            (pair_ref[r].astype(F32) + left[r : r + 1, :] + right).astype(BF16).T for r in some
        ]
        for r, row in zip(some, z):
            z_ref[r] = row
        z = jnp.concatenate(z, axis=1)
        normed = norm_rows(z.astype(F32), gain).astype(BF16)
        operands(normed, half_proj_t, at, sa_ref, sb_ref)
    copy = pltpu.make_async_copy(z_ref, z_out, sem)
    copy.start()
    pack(sa_ref, sb_ref, u_ref)
    copy.wait()


def gate_kernel(layer, z_in, gate_ref, gain_ref, out_ref, z_ref, sem):
    rows, _, tokens = z_ref.shape
    copy = pltpu.make_async_copy(z_in, z_ref, sem)
    copy.start()
    gate_t = gate_ref[layer].T
    gain = column(gain_ref[layer, 0:1, :], tokens)
    copy.wait()
    for r in range(rows):
        z = z_ref[r]
        normed = norm_rows(z.astype(F32), gain).astype(BF16)
        out_ref[r] = sigmoid(mm(gate_t, normed)).astype(BF16)
        out_ref[rows + r] = z


def product_kernel(dims, v_ref, r_ref):
    n, _, length = v_ref.shape
    a = v_ref[:, 0:16, :].astype(F32)
    b = v_ref[:, 16:32, :].astype(F32)
    out = []
    for ch in range(2):
        ac = a[:, ch * 8 : ch * 8 + 8, :].reshape(n * 8, length).astype(BF16)
        bc = b[:, ch * 8 : ch * 8 + 8, :].reshape(n * 8, length).astype(BF16)
        out.append(mm(ac, bc, dims).reshape(n, 8, length))
    r_ref[...] = jnp.concatenate(out, axis=1).astype(BF16)


def update_rows(some, s_ref, out_t, gain, held_ref):
    c, rows = out_t.shape[0], held_ref.shape[0] // 2
    x = jnp.concatenate([get_row(s_ref, r, c) for r in some], axis=1)
    normed = norm_rows(x, gain).astype(BF16)
    gating = jnp.concatenate([held_ref[r].astype(F32) for r in some], axis=1)
    z = jnp.concatenate([held_ref[rows + r].astype(F32) for r in some], axis=1)
    return (z + gating * mm(out_t, normed)).astype(BF16)


def middle_kernel(
    x_ref, held_ref, out_ref, proj_ref, gain_ref,
    z_out, u_ref, s_ref, sa_ref, sb_ref, z_ref, sem,
):
    rows, c, tokens = z_ref.shape
    fill(s_ref, x_ref)
    gain_out = column(gain_ref[0, 1:2, :], GROUP * tokens)
    gain_in = column(gain_ref[1, 0:1, :], GROUP * tokens)
    out_t = out_ref[0].T
    half_proj_t = (proj_ref[1].astype(F32) * 0.5).astype(BF16).T
    for at in range(0, rows, GROUP):
        some = range(at, at + GROUP)
        z = update_rows(some, s_ref, out_t, gain_out, held_ref)
        for k, r in enumerate(some):
            z_ref[r] = z[:, k * tokens : (k + 1) * tokens]
        normed = norm_rows(z.astype(F32), gain_in).astype(BF16)
        operands(normed, half_proj_t, at, sa_ref, sb_ref)
    copy = pltpu.make_async_copy(z_ref, z_out, sem)
    copy.start()
    pack(sa_ref, sb_ref, u_ref)
    copy.wait()


def last_kernel(x_ref, held_ref, out_ref, gain_ref, pair_ref, s_ref):
    rows, tokens, c = pair_ref.shape
    fill(s_ref, x_ref)
    gain_out = column(gain_ref[1, 1:2, :], GROUP * tokens)
    out_t = out_ref[1].T
    for at in range(0, rows, GROUP):
        some = range(at, at + GROUP)
        z = update_rows(some, s_ref, out_t, gain_out, held_ref)
        for k, r in enumerate(some):
            pair_ref[r] = z[:, k * tokens : (k + 1) * tokens].T


def call(
    body, outs, args, scratch=(), name=None, flops=0, bytes_=0, far_in=(), far_out=(), vmem=16
):
    specs = [
        pl.BlockSpec(
            memory_space=pltpu.HBM if k in far_in else pltpu.SMEM if a.ndim == 1 else pltpu.VMEM
        )
        for k, a in enumerate(args)
    ]
    places = [
        pl.BlockSpec(memory_space=pltpu.HBM if k in far_out else pltpu.VMEM)
        for k in range(len(outs))
    ]
    return pl.pallas_call(
        body,
        out_shape=outs,
        in_specs=specs,
        out_specs=places,
        scratch_shapes=list(scratch),
        compiler_params=pltpu.CompilerParams(vmem_limit_bytes=vmem * 2**20),
        cost_estimate=pl.CostEstimate(flops=flops, bytes_accessed=bytes_, transcendentals=0),
        name=name,
    )(*args)


def local(
    pair_map, atom_feats, atom_token, atom_weight, left_weight, right_weight,
    tri_proj, tri_gate, tri_out, tri_gains,
):
    rows, tokens, c = pair_map.shape
    atoms = atom_feats.shape[0]
    cs = atom_weight.shape[1]
    n = lax.axis_size("dap")
    shape = jax.ShapeDtypeStruct
    me = lax.axis_index("dap").astype(jnp.int32).reshape(1)

    ny, nx = 8, 4
    groups_y = [[(y * nx + x) * 2 + k for y in range(ny)] for x in range(nx) for k in range(2)]
    groups_x = [[(y * nx + x) * 2 + k for x in range(nx)] for y in range(ny) for k in range(2)]
    (packed,) = call(
        pack_kernel, (shape((ny, atoms + 16, c), BF16),), (atom_feats, atom_token.reshape(1, atoms)),
        [pltpu.VMEM((atoms, c), BF16), pltpu.VMEM((1, atoms), jnp.int32)]
        + [pltpu.SemaphoreType.DMA] * 2,
        name="packed_atoms", bytes_=300_000, far_in=(0, 1), vmem=60,
    )
    got = lax.all_to_all(
        packed, "dap", split_axis=0, concat_axis=0, tiled=True, axis_index_groups=groups_y
    )
    got = lax.all_gather(got, "dap", axis=0, tiled=True, axis_index_groups=groups_x)
    other = lax.ppermute(got, "dap", [(d, d ^ 1) for d in range(n)])
    (psum,) = call(
        pool_kernel, (shape((tokens, cs + 128), F32),), (got, atom_weight),
        name="pool_half", flops=3_000_000_000, bytes_=2_000_000,
    )
    big = pltpu.VMEM((tokens // 128, rows * c, 128), F32)
    held = [pltpu.VMEM((rows, c, tokens), BF16), pltpu.SemaphoreType.DMA]
    z_shape = shape((rows, c, tokens), BF16)
    sent_shape = shape((n, 32, tokens), BF16)
    token_single, z, sent = call(
        first_kernel,
        (shape((rows, cs), BF16), z_shape, sent_shape),
        (me, psum, other, atom_weight, left_weight, right_weight, pair_map,
         tri_proj, tri_gains),
        [pltpu.VMEM((tokens, cs), F32), big, big, *held],
        name="first", flops=4_000_000_000, bytes_=8_000_000, far_out=(1,), vmem=32,
    )

    def exchange(v):
        return lax.all_to_all(v, "dap", split_axis=0, concat_axis=0, tiled=True)

    for layer in range(2):
        got = exchange(sent)
        (kept,) = call(
            functools.partial(gate_kernel, layer), (shape((2 * rows, c, tokens), BF16),),
            (z, tri_gate, tri_gains), held,
            name=f"gating{layer}", flops=200_000_000, bytes_=3_000_000, far_in=(0,),
        )
        (prod,) = call(
            functools.partial(product_kernel, TN if layer else NT),
            (shape((n, 16, tokens), BF16),), (got,),
            name=f"product{layer}", flops=1_000_000_000, bytes_=3_000_000,
        )
        prod = exchange(prod)
        if layer == 0:
            z, sent = call(
                middle_kernel, (z_shape, sent_shape),
                (prod, kept, tri_out, tri_proj, tri_gains),
                [big, big, big, *held],
                name="middle", flops=1_000_000_000, bytes_=8_000_000, far_out=(0,), vmem=32,
            )
        else:
            (pair,) = call(
                last_kernel, (shape((rows, tokens, c), BF16),),
                (prod, kept, tri_out, tri_gains),
                [big],
                name="last", flops=200_000_000, bytes_=5_000_000,
            )
    return token_single, pair


def solution(mesh):
    placed = (
        P(("dp", "dap"), None, None),
        P(("dp", "dap"), None),
        P(("dp", "dap")),
        P(),
        P(),
        P(),
        P(),
        P(),
        P(),
        P(),
    )
    return jax.shard_map(
        local,
        mesh=mesh,
        in_specs=placed,
        out_specs=(P(("dp", "dap"), None), P(("dp", "dap"), None, None)),
        check_vma=False,
    )
```

```python
import functools

import jax
import jax.numpy as jnp
from jax import lax
from jax.experimental import pallas as pl
from jax.experimental.pallas import tpu as pltpu
from jax.sharding import PartitionSpec as P

EPS = 1e-05
GROUP = 4
PARTS = 2
F32, BF16 = jnp.float32, jnp.bfloat16
NT = (((1,), (1,)), ((), ()))
TN = (((0,), (0,)), ((), ()))
NN = (((1,), (0,)), ((), ()))


def mm(a, b, dims=NN):
    return lax.dot_general(a, b, dims, preferred_element_type=F32)


def sigmoid(x):
    return 0.5 * jnp.tanh(0.5 * x) + 0.5


def column(row, width):
    n = row.shape[1]
    tile = jnp.broadcast_to(row, (128, n)).T
    return jnp.concatenate([tile] * (width // 128), axis=1)


def norm_rows(x, gain):
    n = x.shape[0]
    centred = x - jnp.sum(x, axis=0, keepdims=True) * (1.0 / n)
    variance = jnp.sum(centred * centred, axis=0, keepdims=True) * (1.0 / n)
    return centred * lax.rsqrt(variance + EPS) * gain


def pack_kernel(feats_in, tok_in, out_ref, feats_ref, tok_ref, sem_feats, sem_tok):
    copies = [
        pltpu.make_async_copy(feats_in, feats_ref, sem_feats),
        pltpu.make_async_copy(tok_in, tok_ref, sem_tok),
    ]
    for copy in copies:
        copy.start()
    for copy in copies:
        copy.wait()
    atoms, c = feats_ref.shape
    tok = jnp.concatenate([tok_ref[...], jnp.zeros((1, c - atoms), jnp.int32)], axis=1)
    row = lax.broadcasted_iota(jnp.int32, (16, c), 0)
    codes = jnp.where(row == 0, tok >> 5, jnp.where(row == 1, tok & 31, 0))
    block = jnp.concatenate([feats_ref[...], codes.astype(F32).astype(BF16)], axis=0)
    for k in range(out_ref.shape[0]):
        out_ref[k] = block


def pool(packed_ref, weight_ref, tokens):
    blocks, rows, _ = packed_ref.shape
    atoms = rows - 16
    some = 32
    total = None
    for at in range(0, blocks, some):
        feats = packed_ref[at : at + some, 0:atoms, :].reshape(some * atoms, -1)
        hidden = jnp.maximum(mm(feats, weight_ref[...]), 0.0).astype(BF16)
        hidden = jnp.concatenate([hidden, jnp.ones((some * atoms, 128), BF16)], axis=1)
        toks = []
        for k in range(at, at + some):
            codes = packed_ref[k, atoms:rows, :].astype(F32)
            toks.append((codes[0:1, :atoms] * 32.0 + codes[1:2, :atoms]).astype(jnp.int32))
        toks = jnp.concatenate(toks, axis=1)
        own = lax.broadcasted_iota(jnp.int32, (tokens, some * atoms), 0)
        part = mm(jnp.where(own == toks, 1.0, 0.0).astype(BF16), hidden)
        total = part if total is None else total + part
    return total


def pool_kernel(packed_ref, weight_ref, out_ref):
    out_ref[...] = pool(packed_ref, weight_ref, out_ref.shape[0])


def put_row(s_ref, r, value):
    for t in range(s_ref.shape[0]):
        s_ref[t, pl.ds(r, value.shape[0], stride=8), :] = value[:, t * 128 : t * 128 + 128]


def get_row(s_ref, r, c):
    return jnp.concatenate(
        [s_ref[t, pl.ds(r, c, stride=8), :] for t in range(s_ref.shape[0])], axis=1
    )


def fill(s_ref, x_ref):
    for t in range(s_ref.shape[0]):
        s_ref[t] = x_ref[:, :, t * 128 : t * 128 + 128].reshape(-1, 128).astype(F32)


def operands(normed, half_proj_t, at, sa_ref, sb_ref):
    c = normed.shape[0]
    length = sa_ref.shape[0] * 128
    for s_ref, block in ((sa_ref, 0), (sb_ref, 2)):
        p = mm(half_proj_t[block * c : (block + 2) * c], normed)
        p = jnp.tanh(p[:c]) * p[c:] + p[c:]
        for k in range(normed.shape[1] // length):
            put_row(s_ref, at + k, p[:, k * length : (k + 1) * length])


def pack(sa_ref, sb_ref, u_ref):
    n = u_ref.shape[0]
    for s_ref, at in ((sa_ref, 0), (sb_ref, 16)):
        for t in range(s_ref.shape[0]):
            u_ref[:, at : at + 16, t * 128 : t * 128 + 128] = (
                s_ref[t].reshape(n, 16, 128).astype(BF16)
            )


def first_kernel(
    idx_ref, psum_ref, packed_ref, weight_ref, wl_ref, wr_ref, pair_ref, proj_ref, gain_ref,
    single_ref, z_out, u_ref, ts_ref, sa_ref, sb_ref, z_ref, sem,
):
    rows, tokens, c = pair_ref.shape
    cs = wl_ref.shape[0]
    total = psum_ref[...] + pool(packed_ref, weight_ref, tokens)
    counts = total[:, cs:]
    single = jnp.concatenate(
        [total[:, at : at + 128] / counts for at in range(0, cs, 128)], axis=1
    )
    ts_ref[...] = single
    right = mm(single.astype(BF16), wr_ref[...]).astype(BF16).astype(F32)
    start = pl.multiple_of(idx_ref[0] * 8, 8)
    own = ts_ref[pl.ds(start, 8), :].astype(BF16)
    single_ref[...] = own
    left = mm(own, wl_ref[...]).astype(BF16).astype(F32)
    gain = column(gain_ref[0, 0:1, :], GROUP * tokens)
    half_proj_t = (proj_ref[0].astype(F32) * 0.5).astype(BF16).T
    for at in range(0, rows, GROUP):
        some = range(at, at + GROUP)
        z = [
            (pair_ref[r].astype(F32) + left[r : r + 1, :] + right).astype(BF16).T for r in some
        ]
        for r, row in zip(some, z):
            z_ref[r] = row
        z = jnp.concatenate(z, axis=1)
        normed = norm_rows(z.astype(F32), gain).astype(BF16)
        operands(normed, half_proj_t, at, sa_ref, sb_ref)
    copy = pltpu.make_async_copy(z_ref, z_out, sem)
    copy.start()
    pack(sa_ref, sb_ref, u_ref)
    copy.wait()


def gate_kernel(layer, z_in, gate_ref, gain_ref, out_ref, z_ref, sem):
    rows, _, tokens = z_ref.shape
    copy = pltpu.make_async_copy(z_in, z_ref, sem)
    copy.start()
    gate_t = gate_ref[layer].T
    gain = column(gain_ref[layer, 0:1, :], tokens)
    copy.wait()
    for r in range(rows):
        z = z_ref[r]
        normed = norm_rows(z.astype(F32), gain).astype(BF16)
        out_ref[r] = sigmoid(mm(gate_t, normed)).astype(BF16)
        out_ref[rows + r] = z


def product_kernel(dims, v_ref, r_out, r_ref, sem):
    n, _, length = v_ref.shape
    a = v_ref[:, 0:16, :].astype(F32)
    b = v_ref[:, 16:32, :].astype(F32)
    a = [a[:, k : k + 8, :].reshape(n * 8, length).astype(BF16) for k in (0, 8)]
    b = [b[:, k : k + 8, :].reshape(n * 8, length).astype(BF16) for k in (0, 8)]
    if dims == TN:
        a, dims = [x.T for x in a], NN
    part = n // PARTS
    copies = []
    for k in range(PARTS):
        out = [
            mm(x[k * part * 8 : (k + 1) * part * 8], y, dims).reshape(part, 8, length)
            for x, y in zip(a, b)
        ]
        here = pl.ds(k * part, part)
        r_ref[here] = jnp.concatenate(out, axis=1).astype(BF16)
        copies.append(pltpu.make_async_copy(r_ref.at[here], r_out.at[here], sem.at[k]))
        copies[-1].start()
    for copy in copies:
        copy.wait()


def update_rows(some, s_ref, out_t, gain, held_ref):
    c, rows = out_t.shape[0], held_ref.shape[0] // 2
    x = jnp.concatenate([get_row(s_ref, r, c) for r in some], axis=1)
    normed = norm_rows(x, gain).astype(BF16)
    gating = jnp.concatenate([held_ref[r].astype(F32) for r in some], axis=1)
    z = jnp.concatenate([held_ref[rows + r].astype(F32) for r in some], axis=1)
    return (z + gating * mm(out_t, normed)).astype(BF16)


def middle_kernel(
    x_ref, held_ref, out_ref, proj_ref, gain_ref,
    z_out, u_ref, s_ref, sa_ref, sb_ref, z_ref, sem,
):
    rows, c, tokens = z_ref.shape
    fill(s_ref, x_ref)
    gain_out = column(gain_ref[0, 1:2, :], GROUP * tokens)
    gain_in = column(gain_ref[1, 0:1, :], GROUP * tokens)
    out_t = out_ref[0].T
    half_proj_t = (proj_ref[1].astype(F32) * 0.5).astype(BF16).T
    for at in range(0, rows, GROUP):
        some = range(at, at + GROUP)
        z = update_rows(some, s_ref, out_t, gain_out, held_ref)
        for k, r in enumerate(some):
            z_ref[r] = z[:, k * tokens : (k + 1) * tokens]
        normed = norm_rows(z.astype(F32), gain_in).astype(BF16)
        operands(normed, half_proj_t, at, sa_ref, sb_ref)
    copy = pltpu.make_async_copy(z_ref, z_out, sem)
    copy.start()
    pack(sa_ref, sb_ref, u_ref)
    copy.wait()


def last_kernel(x_ref, held_ref, out_ref, gain_ref, pair_out, s_ref, pair_ref, sem):
    rows, tokens, c = pair_ref.shape
    fill(s_ref, x_ref)
    gain_out = column(gain_ref[1, 1:2, :], GROUP * tokens)
    out_t = out_ref[1].T
    copies = []
    for at in range(0, rows, GROUP):
        some = range(at, at + GROUP)
        z = update_rows(some, s_ref, out_t, gain_out, held_ref)
        for k, r in enumerate(some):
            pair_ref[r] = z[:, k * tokens : (k + 1) * tokens].T
        here = pl.ds(at, GROUP)
        k = at // GROUP
        copies.append(pltpu.make_async_copy(pair_ref.at[here], pair_out.at[here], sem.at[k]))
        copies[-1].start()
    for copy in copies:
        copy.wait()


def call(
    body, outs, args, scratch=(), name=None, flops=0, bytes_=0, far_in=(), far_out=(), vmem=16
):
    specs = [
        pl.BlockSpec(
            memory_space=pltpu.HBM if k in far_in else pltpu.SMEM if a.ndim == 1 else pltpu.VMEM
        )
        for k, a in enumerate(args)
    ]
    places = [
        pl.BlockSpec(memory_space=pltpu.HBM if k in far_out else pltpu.VMEM)
        for k in range(len(outs))
    ]
    return pl.pallas_call(
        body,
        out_shape=outs,
        in_specs=specs,
        out_specs=places,
        scratch_shapes=list(scratch),
        compiler_params=pltpu.CompilerParams(vmem_limit_bytes=vmem * 2**20),
        cost_estimate=pl.CostEstimate(flops=flops, bytes_accessed=bytes_, transcendentals=0),
        name=name,
    )(*args)


def local(
    pair_map, atom_feats, atom_token, atom_weight, left_weight, right_weight,
    tri_proj, tri_gate, tri_out, tri_gains,
):
    rows, tokens, c = pair_map.shape
    atoms = atom_feats.shape[0]
    cs = atom_weight.shape[1]
    n = lax.axis_size("dap")
    shape = jax.ShapeDtypeStruct
    me = lax.axis_index("dap").astype(jnp.int32).reshape(1)

    ny, nx = 8, 4
    groups_y = [[(y * nx + x) * 2 + k for y in range(ny)] for x in range(nx) for k in range(2)]
    groups_x = [[(y * nx + x) * 2 + k for x in range(nx)] for y in range(ny) for k in range(2)]
    (packed,) = call(
        pack_kernel, (shape((ny, atoms + 16, c), BF16),), (atom_feats, atom_token.reshape(1, atoms)),
        [pltpu.VMEM((atoms, c), BF16), pltpu.VMEM((1, atoms), jnp.int32)]
        + [pltpu.SemaphoreType.DMA] * 2,
        name="packed_atoms", bytes_=300_000, far_in=(0, 1), vmem=60,
    )
    got = lax.all_to_all(
        packed, "dap", split_axis=0, concat_axis=0, tiled=True, axis_index_groups=groups_y
    )
    got = lax.all_gather(got, "dap", axis=0, tiled=True, axis_index_groups=groups_x)
    other = lax.ppermute(got, "dap", [(d, d ^ 1) for d in range(n)])
    (psum,) = call(
        pool_kernel, (shape((tokens, cs + 128), F32),), (got, atom_weight),
        name="pool_half", flops=3_000_000_000, bytes_=2_000_000,
    )
    big = pltpu.VMEM((tokens // 128, rows * c, 128), F32)
    held = [pltpu.VMEM((rows, c, tokens), BF16), pltpu.SemaphoreType.DMA]
    z_shape = shape((rows, c, tokens), BF16)
    sent_shape = shape((n, 32, tokens), BF16)
    token_single, z, sent = call(
        first_kernel,
        (shape((rows, cs), BF16), z_shape, sent_shape),
        (me, psum, other, atom_weight, left_weight, right_weight, pair_map,
         tri_proj, tri_gains),
        [pltpu.VMEM((tokens, cs), F32), big, big, *held],
        name="first", flops=4_000_000_000, bytes_=8_000_000, far_out=(1,), vmem=32,
    )

    def exchange(v):
        return lax.all_to_all(v, "dap", split_axis=0, concat_axis=0, tiled=True)

    for layer in range(2):
        got = exchange(sent)
        (kept,) = call(
            functools.partial(gate_kernel, layer), (shape((2 * rows, c, tokens), BF16),),
            (z, tri_gate, tri_gains), held,
            name=f"gating{layer}", flops=200_000_000, bytes_=3_000_000, far_in=(0,),
        )
        (prod,) = call(
            functools.partial(product_kernel, TN if layer else NT),
            (shape((n, 16, tokens), BF16),), (got,),
            [pltpu.VMEM((n, 16, tokens), BF16), pltpu.SemaphoreType.DMA((PARTS,))],
            far_out=(0,), vmem=32, name=f"product{layer}", flops=1_000_000_000, bytes_=3_000_000,
        )
        prod = exchange(prod)
        if layer == 0:
            z, sent = call(
                middle_kernel, (z_shape, sent_shape),
                (prod, kept, tri_out, tri_proj, tri_gains),
                [big, big, big, *held],
                name="middle", flops=1_000_000_000, bytes_=8_000_000, far_out=(0,), vmem=40,
            )
        else:
            (pair,) = call(
                last_kernel, (shape((rows, tokens, c), BF16),),
                (prod, kept, tri_out, tri_gains),
                [big, pltpu.VMEM((rows, tokens, c), BF16), pltpu.SemaphoreType.DMA((rows // GROUP,))],
                far_out=(0,), vmem=32, name="last", flops=200_000_000, bytes_=5_000_000,
            )
    return token_single, pair


def solution(mesh):
    placed = (
        P(("dp", "dap"), None, None),
        P(("dp", "dap"), None),
        P(("dp", "dap")),
        P(),
        P(),
        P(),
        P(),
        P(),
        P(),
        P(),
    )
    return jax.shard_map(
        local,
        mesh=mesh,
        in_specs=placed,
        out_specs=(P(("dp", "dap"), None), P(("dp", "dap"), None, None)),
        check_vma=False,
    )
```

```python
import functools

import jax
import jax.numpy as jnp
from jax import lax
from jax.experimental import pallas as pl
from jax.experimental.pallas import tpu as pltpu
from jax.sharding import PartitionSpec as P

EPS = 1e-05
WIDTH = 128
CODES = 8
PARTS = 2
F32, BF16 = jnp.float32, jnp.bfloat16
NT = (((1,), (1,)), ((), ()))
TN = (((0,), (0,)), ((), ()))
NN = (((1,), (0,)), ((), ()))


def mm(a, b, dims=NN):
    return lax.dot_general(a, b, dims, preferred_element_type=F32)


def sigmoid(x):
    return 0.5 * jnp.tanh(0.5 * x) + 0.5


def column(row, width):
    n = row.shape[1]
    tile = jnp.broadcast_to(row, (128, n)).T
    return jnp.concatenate([tile] * (width // 128), axis=1)


def norm_rows(x, gain):
    n = x.shape[0]
    centred = x - jnp.sum(x, axis=0, keepdims=True) * (1.0 / n)
    variance = jnp.sum(centred * centred, axis=0, keepdims=True) * (1.0 / n)
    return centred * lax.rsqrt(variance + EPS) * gain


def pool(packed_ref, weight_ref, tokens):
    blocks, rows, _ = packed_ref.shape
    atoms = rows - CODES
    some = 32
    total = None
    for at in range(0, blocks, some):
        feats = packed_ref[at : at + some, 0:atoms, :].reshape(some * atoms, -1)
        hidden = jnp.maximum(mm(feats, weight_ref[...]), 0.0).astype(BF16)
        hidden = jnp.concatenate([hidden, jnp.ones((some * atoms, 128), BF16)], axis=1)
        toks = []
        for k in range(at, at + some):
            codes = packed_ref[k, atoms:rows, :].astype(F32)
            toks.append((codes[0:1, :atoms] * 32.0 + codes[1:2, :atoms]).astype(jnp.int32))
        toks = jnp.concatenate(toks, axis=1)
        own = lax.broadcasted_iota(jnp.int32, (tokens, some * atoms), 0)
        part = mm(jnp.where(own == toks, 1.0, 0.0).astype(BF16), hidden)
        total = part if total is None else total + part
    return total


def pool_kernel(packed_ref, weight_ref, out_ref):
    out_ref[...] = pool(packed_ref, weight_ref, out_ref.shape[0])


def put_row(s_ref, r, at, value):
    for k in range(value.shape[1] // 128):
        tile = value[:, k * 128 : k * 128 + 128]
        s_ref[at // 128 + k, pl.ds(r, value.shape[0], stride=8), :] = tile


def get_row(s_ref, r, at, c):
    return jnp.concatenate(
        [s_ref[t, pl.ds(r, c, stride=8), :] for t in range(at // 128, (at + WIDTH) // 128)], axis=1
    )


def fill(s_ref, x_ref):
    for t in range(s_ref.shape[0]):
        s_ref[t] = x_ref[:, :, t * 128 : t * 128 + 128].reshape(-1, 128).astype(F32)


def operands(normed, half_proj_t, at, sa_ref, sb_ref):
    c = normed.shape[0]
    for s_ref, block in ((sa_ref, 0), (sb_ref, 2)):
        p = mm(half_proj_t[block * c : (block + 2) * c], normed)
        p = jnp.tanh(p[:c]) * p[c:] + p[c:]
        for r in range(normed.shape[1] // WIDTH):
            put_row(s_ref, r, at, p[:, r * WIDTH : (r + 1) * WIDTH])


def pack(sa_ref, sb_ref, u_ref):
    n = u_ref.shape[0]
    for s_ref, at in ((sa_ref, 0), (sb_ref, 16)):
        for t in range(s_ref.shape[0]):
            u_ref[:, at : at + 16, t * 128 : t * 128 + 128] = (
                s_ref[t].reshape(n, 16, 128).astype(BF16)
            )


def first_kernel(
    idx_ref, psum_ref, packed_ref, weight_ref, wl_ref, wr_ref, pair_ref, proj_ref, gain_ref,
    single_ref, z_out, u_ref, ts_ref, sa_ref, sb_ref, z_ref, sem,
):
    rows, tokens, c = pair_ref.shape
    cs = wl_ref.shape[0]
    total = psum_ref[...] + pool(packed_ref, weight_ref, tokens)
    counts = total[:, cs:]
    single = jnp.concatenate(
        [total[:, at : at + 128] / counts for at in range(0, cs, 128)], axis=1
    )
    ts_ref[...] = single
    right = mm(single.astype(BF16), wr_ref[...]).astype(BF16).astype(F32)
    start = pl.multiple_of(idx_ref[0] * 8, 8)
    own = ts_ref[pl.ds(start, 8), :].astype(BF16)
    single_ref[...] = own
    left = mm(own, wl_ref[...]).astype(BF16).astype(F32)
    gain = column(gain_ref[0, 0:1, :], rows * WIDTH)
    half_proj_t = (proj_ref[0].astype(F32) * 0.5).astype(BF16).T
    for at in range(0, tokens, WIDTH):
        here = slice(at, at + WIDTH)
        z = [
            (pair_ref[r, here, :].astype(F32) + left[r : r + 1, :] + right[here]).astype(BF16).T
            for r in range(rows)
        ]
        for r, row in enumerate(z):
            z_ref[r, :, here] = row
        z = jnp.concatenate(z, axis=1)
        normed = norm_rows(z.astype(F32), gain).astype(BF16)
        operands(normed, half_proj_t, at, sa_ref, sb_ref)
    copy = pltpu.make_async_copy(z_ref, z_out, sem)
    copy.start()
    pack(sa_ref, sb_ref, u_ref)
    copy.wait()


def gate_kernel(layer, z_in, gate_ref, gain_ref, out_ref, z_ref, sem):
    rows, _, tokens = z_ref.shape
    copy = pltpu.make_async_copy(z_in, z_ref, sem)
    copy.start()
    gate_t = gate_ref[layer].T
    gain = column(gain_ref[layer, 0:1, :], tokens)
    copy.wait()
    for r in range(rows):
        z = z_ref[r]
        normed = norm_rows(z.astype(F32), gain).astype(BF16)
        out_ref[r] = sigmoid(mm(gate_t, normed)).astype(BF16)
        out_ref[rows + r] = z


def product_kernel(dims, v_ref, r_out, r_ref, sem):
    n, _, length = v_ref.shape
    a = v_ref[:, 0:16, :].astype(F32)
    b = v_ref[:, 16:32, :].astype(F32)
    a = [a[:, k : k + 8, :].reshape(n * 8, length).astype(BF16) for k in (0, 8)]
    b = [b[:, k : k + 8, :].reshape(n * 8, length).astype(BF16) for k in (0, 8)]
    if dims == TN:
        a, dims = [x.T for x in a], NN
    part = n // PARTS
    copies = []
    for k in range(PARTS):
        out = [
            mm(x[k * part * 8 : (k + 1) * part * 8], y, dims).reshape(part, 8, length)
            for x, y in zip(a, b)
        ]
        here = pl.ds(k * part, part)
        r_ref[here] = jnp.concatenate(out, axis=1).astype(BF16)
        copies.append(pltpu.make_async_copy(r_ref.at[here], r_out.at[here], sem.at[k]))
        copies[-1].start()
    for copy in copies:
        copy.wait()


def update_rows(at, s_ref, out_t, gain, held_ref):
    c, rows = out_t.shape[0], held_ref.shape[0] // 2
    here = slice(at, at + WIDTH)
    x = jnp.concatenate([get_row(s_ref, r, at, c) for r in range(rows)], axis=1)
    normed = norm_rows(x, gain).astype(BF16)
    gating = jnp.concatenate([held_ref[r, :, here].astype(F32) for r in range(rows)], axis=1)
    z = jnp.concatenate([held_ref[rows + r, :, here].astype(F32) for r in range(rows)], axis=1)
    return (z + gating * mm(out_t, normed)).astype(BF16)


def middle_kernel(
    x_ref, held_ref, out_ref, proj_ref, gain_ref,
    z_out, u_ref, s_ref, sa_ref, sb_ref, z_ref, sem,
):
    rows, c, tokens = z_ref.shape
    fill(s_ref, x_ref)
    gain_out = column(gain_ref[0, 1:2, :], rows * WIDTH)
    gain_in = column(gain_ref[1, 0:1, :], rows * WIDTH)
    out_t = out_ref[0].T
    half_proj_t = (proj_ref[1].astype(F32) * 0.5).astype(BF16).T
    for at in range(0, tokens, WIDTH):
        z = update_rows(at, s_ref, out_t, gain_out, held_ref)
        for r in range(rows):
            z_ref[r, :, at : at + WIDTH] = z[:, r * WIDTH : (r + 1) * WIDTH]
        normed = norm_rows(z.astype(F32), gain_in).astype(BF16)
        operands(normed, half_proj_t, at, sa_ref, sb_ref)
    copy = pltpu.make_async_copy(z_ref, z_out, sem)
    copy.start()
    pack(sa_ref, sb_ref, u_ref)
    copy.wait()


def last_kernel(x_ref, held_ref, out_ref, gain_ref, pair_out, s_ref, pair_ref, sem):
    rows, tokens, c = pair_ref.shape
    fill(s_ref, x_ref)
    gain_out = column(gain_ref[1, 1:2, :], rows * WIDTH)
    out_t = out_ref[1].T
    copies = []
    for at in range(0, tokens, WIDTH):
        z = update_rows(at, s_ref, out_t, gain_out, held_ref)
        for r in range(rows):
            pair_ref[r, at : at + WIDTH, :] = z[:, r * WIDTH : (r + 1) * WIDTH].T
        here = (slice(None), pl.ds(at, WIDTH))
        copies.append(
            pltpu.make_async_copy(pair_ref.at[here], pair_out.at[here], sem.at[at // WIDTH])
        )
        copies[-1].start()
    for copy in copies:
        copy.wait()


def call(
    body, outs, args, scratch=(), name=None, flops=0, bytes_=0, far_in=(), far_out=(), vmem=16
):
    specs = [
        pl.BlockSpec(
            memory_space=pltpu.HBM if k in far_in else pltpu.SMEM if a.ndim == 1 else pltpu.VMEM
        )
        for k, a in enumerate(args)
    ]
    places = [
        pl.BlockSpec(memory_space=pltpu.HBM if k in far_out else pltpu.VMEM)
        for k in range(len(outs))
    ]
    return pl.pallas_call(
        body,
        out_shape=outs,
        in_specs=specs,
        out_specs=places,
        scratch_shapes=list(scratch),
        compiler_params=pltpu.CompilerParams(vmem_limit_bytes=vmem * 2**20),
        cost_estimate=pl.CostEstimate(flops=flops, bytes_accessed=bytes_, transcendentals=0),
        name=name,
    )(*args)


def local(
    pair_map, atom_feats, atom_token, atom_weight, left_weight, right_weight,
    tri_proj, tri_gate, tri_out, tri_gains,
):
    rows, tokens, c = pair_map.shape
    atoms = atom_feats.shape[0]
    cs = atom_weight.shape[1]
    n = lax.axis_size("dap")
    shape = jax.ShapeDtypeStruct
    me = lax.axis_index("dap").astype(jnp.int32).reshape(1)

    ny, nx = 8, 4
    groups_y = [[(y * nx + x) * 2 + k for y in range(ny)] for x in range(nx) for k in range(2)]
    groups_x = [[(y * nx + x) * 2 + k for x in range(nx)] for y in range(ny) for k in range(2)]
    tok = atom_token.reshape(1, atoms)
    tok = jnp.concatenate([tok >> 5, tok & 31], axis=0).astype(BF16)
    tok = jnp.pad(tok, ((0, CODES - 2), (0, c - atoms)))
    packed = jnp.concatenate([atom_feats, tok], axis=0)
    got = lax.all_to_all(
        jnp.broadcast_to(packed[None], (ny,) + packed.shape), "dap", split_axis=0,
        concat_axis=0, tiled=True, axis_index_groups=groups_y,
    )
    got = lax.all_gather(got, "dap", axis=0, tiled=True, axis_index_groups=groups_x)
    other = lax.ppermute(got, "dap", [(d, d ^ 1) for d in range(n)])
    (psum,) = call(
        pool_kernel, (shape((tokens, cs + 128), F32),), (got, atom_weight),
        name="pool_half", flops=3_000_000_000, bytes_=2_000_000,
    )
    big = pltpu.VMEM((tokens // 128, rows * c, 128), F32)
    held = [pltpu.VMEM((rows, c, tokens), BF16), pltpu.SemaphoreType.DMA]
    z_shape = shape((rows, c, tokens), BF16)
    sent_shape = shape((n, 32, tokens), BF16)
    token_single, z, sent = call(
        first_kernel,
        (shape((rows, cs), BF16), z_shape, sent_shape),
        (me, psum, other, atom_weight, left_weight, right_weight, pair_map,
         tri_proj, tri_gains),
        [pltpu.VMEM((tokens, cs), F32), big, big, *held],
        name="first", flops=4_000_000_000, bytes_=8_000_000, far_out=(1,), vmem=32,
    )

    def exchange(v):
        return lax.all_to_all(v, "dap", split_axis=0, concat_axis=0, tiled=True)

    for layer in range(2):
        got = exchange(sent)
        (kept,) = call(
            functools.partial(gate_kernel, layer), (shape((2 * rows, c, tokens), BF16),),
            (z, tri_gate, tri_gains), held,
            name=f"gating{layer}", flops=200_000_000, bytes_=3_000_000, far_in=(0,),
        )
        (prod,) = call(
            functools.partial(product_kernel, TN if layer else NT),
            (shape((n, 16, tokens), BF16),), (got,),
            [pltpu.VMEM((n, 16, tokens), BF16), pltpu.SemaphoreType.DMA((PARTS,))],
            far_out=(0,), vmem=32, name=f"product{layer}", flops=1_000_000_000, bytes_=3_000_000,
        )
        prod = exchange(prod)
        if layer == 0:
            z, sent = call(
                middle_kernel, (z_shape, sent_shape),
                (prod, kept, tri_out, tri_proj, tri_gains),
                [big, big, big, *held],
                name="middle", flops=1_000_000_000, bytes_=8_000_000, far_out=(0,), vmem=40,
            )
        else:
            (pair,) = call(
                last_kernel, (shape((rows, tokens, c), BF16),),
                (prod, kept, tri_out, tri_gains),
                [big, pltpu.VMEM((rows, tokens, c), BF16), pltpu.SemaphoreType.DMA((tokens // WIDTH,))],
                far_out=(0,), vmem=32, name="last", flops=200_000_000, bytes_=5_000_000,
            )
    return token_single, pair


def solution(mesh):
    placed = (
        P(("dp", "dap"), None, None),
        P(("dp", "dap"), None),
        P(("dp", "dap")),
        P(),
        P(),
        P(),
        P(),
        P(),
        P(),
        P(),
    )
    return jax.shard_map(
        local,
        mesh=mesh,
        in_specs=placed,
        out_specs=(P(("dp", "dap"), None), P(("dp", "dap"), None, None)),
        check_vma=False,
    )
```

```python
import functools

import jax
import jax.numpy as jnp
from jax import lax
from jax.experimental import pallas as pl
from jax.experimental.pallas import tpu as pltpu
from jax.sharding import PartitionSpec as P

EPS = 1e-05
WIDTH = 128
CODES = 8
PARTS = 2
F32, BF16 = jnp.float32, jnp.bfloat16
NT = (((1,), (1,)), ((), ()))
TN = (((0,), (0,)), ((), ()))
NN = (((1,), (0,)), ((), ()))


def mm(a, b, dims=NN):
    return lax.dot_general(a, b, dims, preferred_element_type=F32)


def sigmoid(x):
    return 0.5 * jnp.tanh(0.5 * x) + 0.5


def column(row, width):
    n = row.shape[1]
    tile = jnp.broadcast_to(row, (128, n)).T
    return jnp.concatenate([tile] * (width // 128), axis=1)


def norm_rows(x, gain):
    n = x.shape[0]
    centred = x - jnp.sum(x, axis=0, keepdims=True) * (1.0 / n)
    variance = jnp.sum(centred * centred, axis=0, keepdims=True) * (1.0 / n)
    return centred * lax.rsqrt(variance + EPS) * gain


def pack_kernel(feats_in, tok_in, out_ref, feats_ref, tok_ref, sem_feats, sem_tok):
    copies = [
        pltpu.make_async_copy(feats_in, feats_ref, sem_feats),
        pltpu.make_async_copy(tok_in, tok_ref, sem_tok),
    ]
    for copy in copies:
        copy.start()
    for copy in copies:
        copy.wait()
    atoms, c = feats_ref.shape
    tok = jnp.concatenate([tok_ref[...], jnp.zeros((1, c - atoms), jnp.int32)], axis=1)
    row = lax.broadcasted_iota(jnp.int32, (CODES, c), 0)
    codes = jnp.where(row == 0, tok >> 5, jnp.where(row == 1, tok & 31, 0))
    block = jnp.concatenate([feats_ref[...], codes.astype(F32).astype(BF16)], axis=0)
    for k in range(out_ref.shape[0]):
        out_ref[k] = block


def pool(packed_ref, weight_ref, tokens):
    blocks, rows, _ = packed_ref.shape
    atoms = rows - CODES
    some = 32
    total = None
    for at in range(0, blocks, some):
        feats = packed_ref[at : at + some, 0:atoms, :].reshape(some * atoms, -1)
        hidden = jnp.maximum(mm(feats, weight_ref[...].astype(BF16)), 0.0).astype(BF16)
        hidden = jnp.concatenate([hidden, jnp.ones((some * atoms, 128), BF16)], axis=1)
        toks = []
        for k in range(at, at + some):
            codes = packed_ref[k, atoms:rows, :].astype(F32)
            toks.append((codes[0:1, :atoms] * 32.0 + codes[1:2, :atoms]).astype(jnp.int32))
        toks = jnp.concatenate(toks, axis=1)
        own = lax.broadcasted_iota(jnp.int32, (tokens, some * atoms), 0)
        part = mm(jnp.where(own == toks, 1.0, 0.0).astype(BF16), hidden)
        total = part if total is None else total + part
    return total


def pool_kernel(packed_ref, weight_ref, out_ref):
    out_ref[...] = pool(packed_ref, weight_ref, out_ref.shape[0])


def put_row(s_ref, r, at, value):
    for k in range(value.shape[1] // 128):
        tile = value[:, k * 128 : k * 128 + 128]
        s_ref[at // 128 + k, pl.ds(r, value.shape[0], stride=8), :] = tile


def get_row(s_ref, r, at, c):
    return jnp.concatenate(
        [s_ref[t, pl.ds(r, c, stride=8), :] for t in range(at // 128, (at + WIDTH) // 128)], axis=1
    )


def fill(s_ref, x_ref):
    for t in range(s_ref.shape[0]):
        s_ref[t] = x_ref[:, :, t * 128 : t * 128 + 128].reshape(-1, 128).astype(F32)


def operands(normed, half_proj_t, at, sa_ref, sb_ref):
    c = normed.shape[0]
    for s_ref, block in ((sa_ref, 0), (sb_ref, 2)):
        p = mm(half_proj_t[block * c : (block + 2) * c], normed)
        p = jnp.tanh(p[:c]) * p[c:] + p[c:]
        for r in range(normed.shape[1] // WIDTH):
            put_row(s_ref, r, at, p[:, r * WIDTH : (r + 1) * WIDTH])


def pack(sa_ref, sb_ref, u_ref):
    n = u_ref.shape[0]
    for s_ref, at in ((sa_ref, 0), (sb_ref, 16)):
        for t in range(s_ref.shape[0]):
            u_ref[:, at : at + 16, t * 128 : t * 128 + 128] = (
                s_ref[t].reshape(n, 16, 128).astype(BF16)
            )


def first_kernel(
    idx_ref, psum_ref, packed_ref, weight_ref, wl_ref, wr_ref, pair_ref, proj_ref, gain_ref,
    single_ref, z_out, u_ref, ts_ref, sa_ref, sb_ref, z_ref, sem,
):
    rows, tokens, c = pair_ref.shape
    cs = wl_ref.shape[0]
    total = psum_ref[...] + pool(packed_ref, weight_ref, tokens)
    counts = total[:, cs:]
    single = jnp.concatenate(
        [total[:, at : at + 128] / counts for at in range(0, cs, 128)], axis=1
    )
    ts_ref[...] = single
    right = mm(single.astype(BF16), wr_ref[...]).astype(BF16).astype(F32)
    start = pl.multiple_of(idx_ref[0] * 8, 8)
    own = ts_ref[pl.ds(start, 8), :].astype(BF16)
    single_ref[...] = own
    left = mm(own, wl_ref[...]).astype(BF16).astype(F32)
    gain = column(gain_ref[0, 0:1, :], rows * WIDTH)
    half_proj_t = (proj_ref[0].astype(F32) * 0.5).astype(BF16).T
    for at in range(0, tokens, WIDTH):
        here = slice(at, at + WIDTH)
        z = [
            (pair_ref[r, here, :].astype(F32) + left[r : r + 1, :] + right[here]).astype(BF16).T
            for r in range(rows)
        ]
        for r, row in enumerate(z):
            z_ref[r, :, here] = row
        z = jnp.concatenate(z, axis=1)
        normed = norm_rows(z.astype(F32), gain).astype(BF16)
        operands(normed, half_proj_t, at, sa_ref, sb_ref)
    copy = pltpu.make_async_copy(z_ref, z_out, sem)
    copy.start()
    pack(sa_ref, sb_ref, u_ref)
    copy.wait()


def gate_kernel(layer, z_in, gate_ref, gain_ref, out_ref, z_ref, sem):
    rows, _, tokens = z_ref.shape
    copy = pltpu.make_async_copy(z_in, z_ref, sem)
    copy.start()
    gate_t = gate_ref[layer].T
    gain = column(gain_ref[layer, 0:1, :], tokens)
    copy.wait()
    for r in range(rows):
        z = z_ref[r]
        normed = norm_rows(z.astype(F32), gain).astype(BF16)
        out_ref[r] = sigmoid(mm(gate_t, normed)).astype(BF16)
        out_ref[rows + r] = z


def product_kernel(dims, v_ref, r_out, r_ref, sem):
    n, _, length = v_ref.shape
    a = v_ref[:, 0:16, :].astype(F32)
    b = v_ref[:, 16:32, :].astype(F32)
    a = [a[:, k : k + 8, :].reshape(n * 8, length).astype(BF16) for k in (0, 8)]
    b = [b[:, k : k + 8, :].reshape(n * 8, length).astype(BF16) for k in (0, 8)]
    if dims == TN:
        a, dims = [x.T for x in a], NN
    part = n // PARTS
    copies = []
    for k in range(PARTS):
        out = [
            mm(x[k * part * 8 : (k + 1) * part * 8], y, dims).reshape(part, 8, length)
            for x, y in zip(a, b)
        ]
        here = pl.ds(k * part, part)
        r_ref[here] = jnp.concatenate(out, axis=1).astype(BF16)
        copies.append(pltpu.make_async_copy(r_ref.at[here], r_out.at[here], sem.at[k]))
        copies[-1].start()
    for copy in copies:
        copy.wait()


def update_rows(at, s_ref, out_t, gain, held_ref):
    c, rows = out_t.shape[0], held_ref.shape[0] // 2
    here = slice(at, at + WIDTH)
    x = jnp.concatenate([get_row(s_ref, r, at, c) for r in range(rows)], axis=1)
    normed = norm_rows(x, gain).astype(BF16)
    gating = jnp.concatenate([held_ref[r, :, here].astype(F32) for r in range(rows)], axis=1)
    z = jnp.concatenate([held_ref[rows + r, :, here].astype(F32) for r in range(rows)], axis=1)
    return (z + gating * mm(out_t, normed)).astype(BF16)


def middle_kernel(
    x_ref, held_ref, out_ref, proj_ref, gain_ref,
    z_out, u_ref, s_ref, sa_ref, sb_ref, z_ref, sem,
):
    rows, c, tokens = z_ref.shape
    fill(s_ref, x_ref)
    gain_out = column(gain_ref[0, 1:2, :], rows * WIDTH)
    gain_in = column(gain_ref[1, 0:1, :], rows * WIDTH)
    out_t = out_ref[0].T
    half_proj_t = (proj_ref[1].astype(F32) * 0.5).astype(BF16).T
    for at in range(0, tokens, WIDTH):
        z = update_rows(at, s_ref, out_t, gain_out, held_ref)
        for r in range(rows):
            z_ref[r, :, at : at + WIDTH] = z[:, r * WIDTH : (r + 1) * WIDTH]
        normed = norm_rows(z.astype(F32), gain_in).astype(BF16)
        operands(normed, half_proj_t, at, sa_ref, sb_ref)
    copy = pltpu.make_async_copy(z_ref, z_out, sem)
    copy.start()
    pack(sa_ref, sb_ref, u_ref)
    copy.wait()


def last_kernel(x_ref, held_ref, out_ref, gain_ref, pair_out, s_ref, pair_ref, sem):
    rows, tokens, c = pair_ref.shape
    fill(s_ref, x_ref)
    gain_out = column(gain_ref[1, 1:2, :], rows * WIDTH)
    out_t = out_ref[1].T
    copies = []
    for at in range(0, tokens, WIDTH):
        z = update_rows(at, s_ref, out_t, gain_out, held_ref)
        for r in range(rows):
            pair_ref[r, at : at + WIDTH, :] = z[:, r * WIDTH : (r + 1) * WIDTH].T
        here = (slice(None), pl.ds(at, WIDTH))
        copies.append(
            pltpu.make_async_copy(pair_ref.at[here], pair_out.at[here], sem.at[at // WIDTH])
        )
        copies[-1].start()
    for copy in copies:
        copy.wait()


def call(
    body, outs, args, scratch=(), name=None, flops=0, bytes_=0, far_in=(), far_out=(), vmem=16
):
    specs = [
        pl.BlockSpec(
            memory_space=pltpu.HBM if k in far_in else pltpu.SMEM if a.ndim == 1 else pltpu.VMEM
        )
        for k, a in enumerate(args)
    ]
    places = [
        pl.BlockSpec(memory_space=pltpu.HBM if k in far_out else pltpu.VMEM)
        for k in range(len(outs))
    ]
    return pl.pallas_call(
        body,
        out_shape=outs,
        in_specs=specs,
        out_specs=places,
        scratch_shapes=list(scratch),
        compiler_params=pltpu.CompilerParams(vmem_limit_bytes=vmem * 2**20),
        cost_estimate=pl.CostEstimate(flops=flops, bytes_accessed=bytes_, transcendentals=0),
        name=name,
    )(*args)


def local(
    pair_map, atom_feats, atom_token, atom_weight, left_weight, right_weight,
    tri_proj, tri_gate, tri_out, tri_gains,
):
    rows, tokens, c = pair_map.shape
    atoms = atom_feats.shape[0]
    cs = atom_weight.shape[1]
    n = lax.axis_size("dap")
    shape = jax.ShapeDtypeStruct
    me = lax.axis_index("dap").astype(jnp.int32).reshape(1)

    ny, nx = 8, 4
    groups_y = [[(y * nx + x) * 2 + k for y in range(ny)] for x in range(nx) for k in range(2)]
    groups_x = [[(y * nx + x) * 2 + k for x in range(nx)] for y in range(ny) for k in range(2)]
    (packed,) = call(
        pack_kernel, (shape((ny, atoms + CODES, c), BF16),), (atom_feats, atom_token.reshape(1, atoms)),
        [pltpu.VMEM((atoms, c), BF16), pltpu.VMEM((1, atoms), jnp.int32)]
        + [pltpu.SemaphoreType.DMA] * 2,
        name="packed_atoms", bytes_=300_000, far_in=(0, 1), vmem=60,
    )
    got = lax.all_to_all(
        packed, "dap", split_axis=0,
        concat_axis=0, tiled=True, axis_index_groups=groups_y,
    )
    got, weight = lax.optimization_barrier((got, atom_weight.astype(F32)))
    got = lax.all_gather(got, "dap", axis=0, tiled=True, axis_index_groups=groups_x)
    other = lax.ppermute(got, "dap", [(d, d ^ 1) for d in range(n)])
    (psum,) = call(
        pool_kernel, (shape((tokens, cs + 128), F32),), (got, weight),
        name="pool_half", flops=3_000_000_000, bytes_=2_000_000,
    )
    big = pltpu.VMEM((tokens // 128, rows * c, 128), F32)
    held = [pltpu.VMEM((rows, c, tokens), BF16), pltpu.SemaphoreType.DMA]
    z_shape = shape((rows, c, tokens), BF16)
    sent_shape = shape((n, 32, tokens), BF16)
    token_single, z, sent = call(
        first_kernel,
        (shape((rows, cs), BF16), z_shape, sent_shape),
        (me, psum, other, weight, left_weight, right_weight, pair_map,
         tri_proj, tri_gains),
        [pltpu.VMEM((tokens, cs), F32), big, big, *held],
        name="first", flops=4_000_000_000, bytes_=8_000_000, far_out=(1,), vmem=32,
    )

    def exchange(v):
        return lax.all_to_all(v, "dap", split_axis=0, concat_axis=0, tiled=True)

    for layer in range(2):
        got = exchange(sent)
        (kept,) = call(
            functools.partial(gate_kernel, layer), (shape((2 * rows, c, tokens), BF16),),
            (z, tri_gate, tri_gains), held,
            name=f"gating{layer}", flops=200_000_000, bytes_=3_000_000, far_in=(0,),
        )
        (prod,) = call(
            functools.partial(product_kernel, TN if layer else NT),
            (shape((n, 16, tokens), BF16),), (got,),
            [pltpu.VMEM((n, 16, tokens), BF16), pltpu.SemaphoreType.DMA((PARTS,))],
            far_out=(0,), vmem=32, name=f"product{layer}", flops=1_000_000_000, bytes_=3_000_000,
        )
        prod = exchange(prod)
        if layer == 0:
            z, sent = call(
                middle_kernel, (z_shape, sent_shape),
                (prod, kept, tri_out, tri_proj, tri_gains),
                [big, big, big, *held],
                name="middle", flops=1_000_000_000, bytes_=8_000_000, far_out=(0,), vmem=40,
            )
        else:
            (pair,) = call(
                last_kernel, (shape((rows, tokens, c), BF16),),
                (prod, kept, tri_out, tri_gains),
                [big, pltpu.VMEM((rows, tokens, c), BF16), pltpu.SemaphoreType.DMA((tokens // WIDTH,))],
                far_out=(0,), vmem=32, name="last", flops=200_000_000, bytes_=5_000_000,
            )
    return token_single, pair


def solution(mesh):
    placed = (
        P(("dp", "dap"), None, None),
        P(("dp", "dap"), None),
        P(("dp", "dap")),
        P(),
        P(),
        P(),
        P(),
        P(),
        P(),
        P(),
    )
    return jax.shard_map(
        local,
        mesh=mesh,
        in_specs=placed,
        out_specs=(P(("dp", "dap"), None), P(("dp", "dap"), None, None)),
        check_vma=False,
    )
```

```python
import functools

import jax
import jax.numpy as jnp
from jax import lax
from jax.experimental import pallas as pl
from jax.experimental.pallas import tpu as pltpu
from jax.sharding import PartitionSpec as P

EPS = 1e-05
WIDTH = 128
CODES = 8
PARTS = 2
F32, BF16 = jnp.float32, jnp.bfloat16
NT = (((1,), (1,)), ((), ()))
TN = (((0,), (0,)), ((), ()))
NN = (((1,), (0,)), ((), ()))


def mm(a, b, dims=NN):
    return lax.dot_general(a, b, dims, preferred_element_type=F32)


def sigmoid(x):
    return 0.5 * jnp.tanh(0.5 * x) + 0.5


def column(row, width):
    n = row.shape[1]
    tile = jnp.broadcast_to(row, (128, n)).T
    return jnp.concatenate([tile] * (width // 128), axis=1)


def norm_rows(x, gain):
    n = x.shape[0]
    centred = x - jnp.sum(x, axis=0, keepdims=True) * (1.0 / n)
    variance = jnp.sum(centred * centred, axis=0, keepdims=True) * (1.0 / n)
    return centred * lax.rsqrt(variance + EPS) * gain


def pack_kernel(feats_in, tok_in, out_ref, feats_ref, tok_ref, sem_feats, sem_tok):
    copies = [
        pltpu.make_async_copy(feats_in, feats_ref, sem_feats),
        pltpu.make_async_copy(tok_in, tok_ref, sem_tok),
    ]
    for copy in copies:
        copy.start()
    for copy in copies:
        copy.wait()
    atoms, c = feats_ref.shape
    tok = jnp.concatenate([tok_ref[...], jnp.zeros((1, c - atoms), jnp.int32)], axis=1)
    row = lax.broadcasted_iota(jnp.int32, (CODES, c), 0)
    codes = jnp.where(row == 0, tok >> 5, jnp.where(row == 1, tok & 31, 0))
    block = jnp.concatenate([feats_ref[...], codes.astype(F32).astype(BF16)], axis=0)
    for k in range(out_ref.shape[0]):
        out_ref[k] = block


def pool(packed_ref, weight_ref, tokens):
    blocks, rows, _ = packed_ref.shape
    atoms = rows - CODES
    some = 32
    total = None
    for at in range(0, blocks, some):
        feats = packed_ref[at : at + some, 0:atoms, :].reshape(some * atoms, -1)
        hidden = jnp.maximum(mm(feats, weight_ref[...].astype(BF16)), 0.0).astype(BF16)
        hidden = jnp.concatenate([hidden, jnp.ones((some * atoms, 128), BF16)], axis=1)
        toks = []
        for k in range(at, at + some):
            codes = packed_ref[k, atoms:rows, :].astype(F32)
            toks.append((codes[0:1, :atoms] * 32.0 + codes[1:2, :atoms]).astype(jnp.int32))
        toks = jnp.concatenate(toks, axis=1)
        own = lax.broadcasted_iota(jnp.int32, (tokens, some * atoms), 0)
        part = mm(jnp.where(own == toks, 1.0, 0.0).astype(BF16), hidden)
        total = part if total is None else total + part
    return total


def pool_kernel(packed_ref, weight_ref, out_ref):
    out_ref[...] = pool(packed_ref, weight_ref, out_ref.shape[0])


def put_row(s_ref, r, at, value):
    for k in range(value.shape[1] // 128):
        tile = value[:, k * 128 : k * 128 + 128]
        s_ref[at // 128 + k, pl.ds(r, value.shape[0], stride=8), :] = tile


def get_row(s_ref, r, at, c):
    return jnp.concatenate(
        [s_ref[t, pl.ds(r, c, stride=8), :] for t in range(at // 128, (at + WIDTH) // 128)], axis=1
    )


def fill(s_ref, x_ref):
    for t in range(s_ref.shape[0]):
        s_ref[t] = x_ref[:, :, t * 128 : t * 128 + 128].reshape(-1, 128).astype(F32)


def operands(normed, half_proj_t, at, sa_ref, sb_ref):
    c = normed.shape[0]
    for s_ref, block in ((sa_ref, 0), (sb_ref, 2)):
        p = mm(half_proj_t[block * c : (block + 2) * c], normed)
        p = jnp.tanh(p[:c]) * p[c:] + p[c:]
        for r in range(normed.shape[1] // WIDTH):
            put_row(s_ref, r, at, p[:, r * WIDTH : (r + 1) * WIDTH])


def pack(sa_ref, sb_ref, u_ref):
    n = u_ref.shape[0]
    for s_ref, at in ((sa_ref, 0), (sb_ref, 16)):
        for t in range(s_ref.shape[0]):
            u_ref[:, at : at + 16, t * 128 : t * 128 + 128] = (
                s_ref[t].reshape(n, 16, 128).astype(BF16)
            )


def first_kernel(
    idx_ref, psum_ref, packed_ref, weight_ref, wl_ref, wr_ref, pair_ref, proj_ref, gain_ref,
    single_ref, z_out, u_ref, ts_ref, sa_ref, sb_ref, z_ref, sem,
):
    rows, tokens, c = pair_ref.shape
    cs = wl_ref.shape[0]
    total = psum_ref[...] + pool(packed_ref, weight_ref, tokens)
    share = 1.0 / total[:, cs:]
    single = jnp.concatenate(
        [total[:, at : at + 128] * share for at in range(0, cs, 128)], axis=1
    )
    ts_ref[...] = single
    right = mm(single.astype(BF16), wr_ref[...]).astype(BF16).astype(F32)
    start = pl.multiple_of(idx_ref[0] * 8, 8)
    own = ts_ref[pl.ds(start, 8), :].astype(BF16)
    single_ref[...] = own
    left = mm(own, wl_ref[...]).astype(BF16).astype(F32)
    gain = column(gain_ref[0, 0:1, :], rows * WIDTH)
    half_proj_t = (proj_ref[0].astype(F32) * 0.5).astype(BF16).T
    for at in range(0, tokens, WIDTH):
        here = slice(at, at + WIDTH)
        z = [
            (pair_ref[r, here, :].astype(F32) + left[r : r + 1, :] + right[here]).astype(BF16).T
            for r in range(rows)
        ]
        for r, row in enumerate(z):
            z_ref[r, :, here] = row
        z = jnp.concatenate(z, axis=1)
        normed = norm_rows(z.astype(F32), gain).astype(BF16)
        operands(normed, half_proj_t, at, sa_ref, sb_ref)
    copy = pltpu.make_async_copy(z_ref, z_out, sem)
    copy.start()
    pack(sa_ref, sb_ref, u_ref)
    copy.wait()


def gate_kernel(layer, z_in, gate_ref, gain_ref, out_ref, z_ref, sem):
    rows, _, tokens = z_ref.shape
    copy = pltpu.make_async_copy(z_in, z_ref, sem)
    copy.start()
    gate_t = gate_ref[layer].T
    gain = column(gain_ref[layer, 0:1, :], tokens)
    copy.wait()
    for r in range(rows):
        z = z_ref[r]
        normed = norm_rows(z.astype(F32), gain).astype(BF16)
        out_ref[r] = sigmoid(mm(gate_t, normed)).astype(BF16)
        out_ref[rows + r] = z


def product_kernel(dims, v_ref, r_out, r_ref, sem):
    n, _, length = v_ref.shape
    a = v_ref[:, 0:16, :].astype(F32)
    b = v_ref[:, 16:32, :].astype(F32)
    a = [a[:, k : k + 8, :].reshape(n * 8, length).astype(BF16) for k in (0, 8)]
    b = [b[:, k : k + 8, :].reshape(n * 8, length).astype(BF16) for k in (0, 8)]
    if dims == TN:
        a, dims = [x.T for x in a], NN
    part = n // PARTS
    copies = []
    for k in range(PARTS):
        out = [
            mm(x[k * part * 8 : (k + 1) * part * 8], y, dims).reshape(part, 8, length)
            for x, y in zip(a, b)
        ]
        here = pl.ds(k * part, part)
        r_ref[here] = jnp.concatenate(out, axis=1).astype(BF16)
        copies.append(pltpu.make_async_copy(r_ref.at[here], r_out.at[here], sem.at[k]))
        copies[-1].start()
    for copy in copies:
        copy.wait()


def update_rows(at, s_ref, out_t, gain, held_ref):
    c, rows = out_t.shape[0], held_ref.shape[0] // 2
    here = slice(at, at + WIDTH)
    x = jnp.concatenate([get_row(s_ref, r, at, c) for r in range(rows)], axis=1)
    normed = norm_rows(x, gain).astype(BF16)
    gating = jnp.concatenate([held_ref[r, :, here].astype(F32) for r in range(rows)], axis=1)
    z = jnp.concatenate([held_ref[rows + r, :, here].astype(F32) for r in range(rows)], axis=1)
    return (z + gating * mm(out_t, normed)).astype(BF16)


def middle_kernel(
    x_ref, held_ref, out_ref, proj_ref, gain_ref,
    z_out, u_ref, s_ref, sa_ref, sb_ref, z_ref, sem,
):
    rows, c, tokens = z_ref.shape
    fill(s_ref, x_ref)
    gain_out = column(gain_ref[0, 1:2, :], rows * WIDTH)
    gain_in = column(gain_ref[1, 0:1, :], rows * WIDTH)
    out_t = out_ref[0].T
    half_proj_t = (proj_ref[1].astype(F32) * 0.5).astype(BF16).T
    for at in range(0, tokens, WIDTH):
        z = update_rows(at, s_ref, out_t, gain_out, held_ref)
        for r in range(rows):
            z_ref[r, :, at : at + WIDTH] = z[:, r * WIDTH : (r + 1) * WIDTH]
        normed = norm_rows(z.astype(F32), gain_in).astype(BF16)
        operands(normed, half_proj_t, at, sa_ref, sb_ref)
    copy = pltpu.make_async_copy(z_ref, z_out, sem)
    copy.start()
    pack(sa_ref, sb_ref, u_ref)
    copy.wait()


def last_kernel(x_ref, held_ref, out_ref, gain_ref, pair_out, s_ref, pair_ref, sem):
    rows, tokens, c = pair_ref.shape
    fill(s_ref, x_ref)
    gain_out = column(gain_ref[1, 1:2, :], rows * WIDTH)
    out_t = out_ref[1].T
    copies = []
    for at in range(0, tokens, WIDTH):
        z = update_rows(at, s_ref, out_t, gain_out, held_ref)
        for r in range(rows):
            pair_ref[r, at : at + WIDTH, :] = z[:, r * WIDTH : (r + 1) * WIDTH].T
        here = (slice(None), pl.ds(at, WIDTH))
        copies.append(
            pltpu.make_async_copy(pair_ref.at[here], pair_out.at[here], sem.at[at // WIDTH])
        )
        copies[-1].start()
    for copy in copies:
        copy.wait()


def call(
    body, outs, args, scratch=(), name=None, flops=0, bytes_=0, far_in=(), far_out=(), vmem=16
):
    specs = [
        pl.BlockSpec(
            memory_space=pltpu.HBM if k in far_in else pltpu.SMEM if a.ndim == 1 else pltpu.VMEM
        )
        for k, a in enumerate(args)
    ]
    places = [
        pl.BlockSpec(memory_space=pltpu.HBM if k in far_out else pltpu.VMEM)
        for k in range(len(outs))
    ]
    return pl.pallas_call(
        body,
        out_shape=outs,
        in_specs=specs,
        out_specs=places,
        scratch_shapes=list(scratch),
        compiler_params=pltpu.CompilerParams(vmem_limit_bytes=vmem * 2**20),
        cost_estimate=pl.CostEstimate(flops=flops, bytes_accessed=bytes_, transcendentals=0),
        name=name,
    )(*args)


def local(
    pair_map, atom_feats, atom_token, atom_weight, left_weight, right_weight,
    tri_proj, tri_gate, tri_out, tri_gains,
):
    rows, tokens, c = pair_map.shape
    atoms = atom_feats.shape[0]
    cs = atom_weight.shape[1]
    n = lax.axis_size("dap")
    shape = jax.ShapeDtypeStruct
    me = lax.axis_index("dap").astype(jnp.int32).reshape(1)

    ny, nx = 8, 4
    groups_y = [[(y * nx + x) * 2 + k for y in range(ny)] for x in range(nx) for k in range(2)]
    groups_x = [[(y * nx + x) * 2 + k for x in range(nx)] for y in range(ny) for k in range(2)]
    (packed,) = call(
        pack_kernel, (shape((ny, atoms + CODES, c), BF16),), (atom_feats, atom_token.reshape(1, atoms)),
        [pltpu.VMEM((atoms, c), BF16), pltpu.VMEM((1, atoms), jnp.int32)]
        + [pltpu.SemaphoreType.DMA] * 2,
        name="packed_atoms", bytes_=300_000, far_in=(0, 1), vmem=60,
    )
    got = lax.all_to_all(
        packed, "dap", split_axis=0,
        concat_axis=0, tiled=True, axis_index_groups=groups_y,
    )
    got, weight = lax.optimization_barrier((got, atom_weight.astype(F32)))
    got = lax.all_gather(got, "dap", axis=0, tiled=True, axis_index_groups=groups_x)
    other = lax.ppermute(got, "dap", [(d, d ^ 1) for d in range(n)])
    (psum,) = call(
        pool_kernel, (shape((tokens, cs + 128), F32),), (got, weight),
        name="pool_half", flops=3_000_000_000, bytes_=2_000_000,
    )
    big = pltpu.VMEM((tokens // 128, rows * c, 128), F32)
    held = [pltpu.VMEM((rows, c, tokens), BF16), pltpu.SemaphoreType.DMA]
    z_shape = shape((rows, c, tokens), BF16)
    sent_shape = shape((n, 32, tokens), BF16)
    token_single, z, sent = call(
        first_kernel,
        (shape((rows, cs), BF16), z_shape, sent_shape),
        (me, psum, other, weight, left_weight, right_weight, pair_map,
         tri_proj, tri_gains),
        [pltpu.VMEM((tokens, cs), F32), big, big, *held],
        name="first", flops=4_000_000_000, bytes_=8_000_000, far_out=(1,), vmem=32,
    )

    def exchange(v):
        return lax.all_to_all(v, "dap", split_axis=0, concat_axis=0, tiled=True)

    for layer in range(2):
        got = exchange(sent)
        (kept,) = call(
            functools.partial(gate_kernel, layer), (shape((2 * rows, c, tokens), BF16),),
            (z, tri_gate, tri_gains), held,
            name=f"gating{layer}", flops=200_000_000, bytes_=3_000_000, far_in=(0,),
        )
        (prod,) = call(
            functools.partial(product_kernel, TN if layer else NT),
            (shape((n, 16, tokens), BF16),), (got,),
            [pltpu.VMEM((n, 16, tokens), BF16), pltpu.SemaphoreType.DMA((PARTS,))],
            far_out=(0,), vmem=32, name=f"product{layer}", flops=1_000_000_000, bytes_=3_000_000,
        )
        prod = exchange(prod)
        if layer == 0:
            z, sent = call(
                middle_kernel, (z_shape, sent_shape),
                (prod, kept, tri_out, tri_proj, tri_gains),
                [big, big, big, *held],
                name="middle", flops=1_000_000_000, bytes_=8_000_000, far_out=(0,), vmem=40,
            )
        else:
            (pair,) = call(
                last_kernel, (shape((rows, tokens, c), BF16),),
                (prod, kept, tri_out, tri_gains),
                [big, pltpu.VMEM((rows, tokens, c), BF16), pltpu.SemaphoreType.DMA((tokens // WIDTH,))],
                far_out=(0,), vmem=32, name="last", flops=200_000_000, bytes_=5_000_000,
            )
    return token_single, pair


def solution(mesh):
    placed = (
        P(("dp", "dap"), None, None),
        P(("dp", "dap"), None),
        P(("dp", "dap")),
        P(),
        P(),
        P(),
        P(),
        P(),
        P(),
        P(),
    )
    return jax.shard_map(
        local,
        mesh=mesh,
        in_specs=placed,
        out_specs=(P(("dp", "dap"), None), P(("dp", "dap"), None, None)),
        check_vma=False,
    )
```
